128 devices in a mesh: row: 8 (over y_lo, z), col: 16 (over x, y_hi, core).
Axes of the slice: x: 4, y: 4 (y_hi: 2, y_lo: 2; y = y_hi * 2 + y_lo), z: 4, core: 2. Of those that a mesh axis runs over, the one named last changes fastest.
Arguments:
- layer_input: bfloat16 [8192, 7168], P('row', 'col'), may hold values from -6 to 6
- output_grad: bfloat16 [8192, 7168], P('row', 'col'), may hold values from -6 to 6
- gate_pre: bfloat16 [8192, 4864], P('row', 'col'), may hold values from -8 to 8
- up_pre: bfloat16 [8192, 4864], P('row', 'col'), may hold values from -6 to 6
- down_weight: bfloat16 [4864, 7168], P('col', 'row'), may hold values from -0.078125 to 0.078125
- route_ids: int32 [8192, 2], P('row'), may hold values from 0 to 127, all different within a row; in each aligned block of 1024 rows (0 to 1023, 1024 to 2047, ...) at most 24 rows name the same one
- route_gates: float32 [8192, 2], P('row'), may hold values from 0.2 to 1
- expert_gate: bfloat16 [8, 7168, 2432], P('row', None, 'col'), may hold values from -0.0625 to 0.0625
- expert_up: bfloat16 [8, 7168, 2432], P('row', None, 'col'), may hold values from -0.0625 to 0.0625
- expert_down: bfloat16 [8, 2432, 7168], P('row', 'col'), may hold values from -0.078125 to 0.078125
Outputs:
- gate_pre_grad: bfloat16 [8192, 4864], P('row', 'col')
- up_pre_grad: bfloat16 [8192, 4864], P('row', 'col')
- down_weight_grad: bfloat16 [4864, 7168], P('col', 'row')
- expert_gate_grad: bfloat16 [8, 7168, 2432], P('row', None, 'col')
- expert_up_grad: bfloat16 [8, 7168, 2432], P('row', None, 'col')
- expert_down_grad: bfloat16 [8, 2432, 7168], P('row', 'col')
- moe_input_grad: bfloat16 [8192, 7168], P('row', 'col')
The draws below stay inside these ranges and needn't reach their ends.
Inputs may be any that keep to these rules, and one draw needn't show every extreme that they name: `route_ids`: each row names two different experts. Among the 1024 rows of one index of row, no expert is named by more than 24 rows, a bound that some block reaches.
All inputs are finite; a program needn't handle non-finite values.
Results may differ from the reference program's by a relative error of at most 0.02.
Values may be sent and summed in bfloat16 or wider, within the bound.
A program may use at most 192 MiB of HBM per device.

```python
import math
import jax
import jax.numpy as jnp
import numpy as np
from jax import lax

D = 7168
FF = 4864
EXPERTS = 128
TOK_ROW = 1024
CAP = 24
TOKENS = 8192
N_ROW = 8


def block_scale(stream_key, extent, cuts, least, largest):
    level, own = 1.0, jax.random.fold_in(stream_key, 6)
    for position, shards_of in cuts:
        steps = jnp.exp(jax.random.uniform(jax.random.fold_in(own, position), (shards_of,), jnp.float32, least / len(cuts), largest / len(cuts)))
        level = level * jnp.repeat(steps, extent[position] // shards_of).reshape([-1 if axis == position else 1 for axis in range(len(extent))])
    return level


def shared_out(own_key, own, number, rows, number_of, top, limit, slope):
    order = jax.random.permutation(own_key, number_of)
    packed, ordinary = shares(number_of, rows * top, limit, slope, True), shares(number_of, rows * top, limit, slope, False)
    places = jnp.arange(number_of)

    def named(lengths, offset_by):
        used = int((lengths > 0).sum())
        fixed = max(1, used // 4)
        shifted = fixed + (places - fixed + offset_by * (used - fixed)) % max(1, number_of - fixed)
        return jnp.zeros((number_of,), jnp.int32).at[order[jnp.where(places < fixed, places, shifted)]].set(jnp.asarray(lengths, jnp.int32))

    lengths = jnp.where(number % 4 == 0, named(packed, number // 4), named(ordinary, number - number // 4 - 1))
    mixed = jax.random.permutation(jax.random.fold_in(own, 3), number_of)
    donor, taker = mixed[0:number_of // 2 * 2:2], mixed[1:number_of // 2 * 2:2]
    margin = jnp.minimum(lengths[donor] - 1, limit - lengths[taker]) // 2
    margin = jnp.where((donor == order[0]) | (taker == order[0]) | (lengths[taker] == 0), 0, jnp.maximum(margin, 0))
    shifted = jax.random.randint(jax.random.fold_in(own, 4), (number_of // 2,), 0, 1 << 20) % (margin + 1)
    lengths = lengths.at[donor].add(-shifted).at[taker].add(shifted)
    items = jnp.searchsorted(jnp.cumsum(lengths), jnp.arange(rows * top), side="right").astype(jnp.int32)
    table = items.reshape(top, rows).T
    table = table[jax.random.permutation(jax.random.fold_in(own, 1), rows)]
    offset_by = jax.random.randint(jax.random.fold_in(own, 2), (rows, 1), 0, top)
    return jnp.take_along_axis(table, (jnp.arange(top)[None, :] + offset_by) % top, axis=1)


def shares(amount, total, reach, skew, full):
    weights = [(1 << 20) // math.isqrt(standing ** skew) + 1 for standing in range(1, amount + 1)]
    largest = reach if full else min(reach, max(-(-total // amount), total * weights[0] // sum(weights)))
    least = 1 if total - largest >= amount - 1 else 0
    counts, rest = [largest] + [least] * (amount - 1), total - largest - least * (amount - 1)
    while rest > 0:
        candidates = [i for i in range(1, amount) if counts[i] < largest] or [i for i in range(1, amount) if counts[i] < reach]
        mass, left = sum([weights[i] for i in candidates]), rest
        for i in candidates:
            addition = min(reach - counts[i], max(1, left * weights[i] // mass), rest)
            counts[i] = counts[i] + addition
            rest = rest - addition
    return np.array(counts)


def bell_draw(own_key, extent, deviation, bound, shards=(), kind=jnp.bfloat16):
    result = deviation * jax.random.normal(own_key, extent, jnp.float32)
    if shards:
        result = result * block_scale(own_key, extent, shards, -0.22, 0.18)
    return jnp.clip(result, -bound, bound).astype(kind)


def setup_inputs(seed: int = 0) -> dict:
    key_of = jax.random.split(jax.random.key(seed), 11)
    layer_input = bell_draw(key_of[0], (TOKENS, D), 1.0, 6.0, ((0, 8), (1, 16)))
    output_grad = bell_draw(key_of[1], (TOKENS, D), 1.0, 6.0, ((0, 8), (1, 16)))
    gate_pre = bell_draw(key_of[2], (TOKENS, FF), 1.5, 8.0, ((0, 8), (1, 16)))
    up_pre = bell_draw(key_of[3], (TOKENS, FF), 1.0, 6.0, ((0, 8), (1, 16)))
    down_weight = bell_draw(key_of[4], (FF, D), FF ** -0.5, 0.078125, ((0, 16), (1, 8)))
    route_ids_keys = jax.random.split(jax.random.fold_in(key_of[5], 1), TOKENS // TOK_ROW)
    route_ids_turns = jax.random.permutation(jax.random.fold_in(key_of[5], 3), TOKENS // TOK_ROW)
    route_ids = jax.vmap(lambda own, number: shared_out(jax.random.fold_in(key_of[5], 2), own, number, TOK_ROW, EXPERTS, 2, CAP, 2))(route_ids_keys, route_ids_turns).reshape((TOKENS, 2))
    route_gates = jnp.clip(0.2 + 0.8 * jax.random.uniform(key_of[6], (TOKENS, 2), jnp.float32) ** block_scale(key_of[6], (TOKENS, 2), ((0, 8),), -0.2, 0.2), 0.2, 1.0)
    expert_gate = bell_draw(key_of[7], (N_ROW, D, FF // 2), D ** -0.5, 0.0625, ((0, 8), (2, 16)))
    expert_up = bell_draw(key_of[8], (N_ROW, D, FF // 2), D ** -0.5, 0.0625, ((0, 8), (2, 16)))
    expert_down = bell_draw(key_of[9], (N_ROW, FF // 2, D), FF ** -0.5, 0.078125, ((0, 8), (1, 16)))
    return {"layer_input": layer_input, "output_grad": output_grad, "gate_pre": gate_pre, "up_pre": up_pre, "down_weight": down_weight, "route_ids": route_ids, "route_gates": route_gates, "expert_gate": expert_gate, "expert_up": expert_up, "expert_down": expert_down}


def silu_slope(values):
    sigma = jax.nn.sigmoid(values)
    return sigma * (1.0 + values * (1.0 - sigma))


def slot_tables(route_block, gate_block, windows, capacity):
    count = route_block.shape[0]
    routes = route_block.reshape(-1)
    experts = jnp.arange(windows, dtype=jnp.int32)
    hits = (routes[:, None] == experts[None, :]).astype(jnp.int32)
    ranks = jnp.cumsum(hits, axis=0) - hits
    places = jnp.arange(capacity, dtype=jnp.int32)
    matched = hits[:, :, None] * (ranks[:, :, None] == places[None, None, :]).astype(jnp.int32)
    matched = matched.reshape(count, 2, windows, capacity).astype(jnp.float32)
    picked = jnp.sum(matched, axis=1)
    weighed = jnp.einsum("tkec,tk->ec", matched, gate_block.astype(jnp.float32), precision=lax.Precision.HIGHEST)
    return picked, weighed


def reference(layer_input, output_grad, gate_pre, up_pre, down_weight, route_ids, route_gates, expert_gate, expert_up, expert_down):
    gate_float = gate_pre.astype(jnp.float32)
    up_float = up_pre.astype(jnp.float32)
    activated = jax.nn.silu(gate_float)
    hidden = (activated * up_float).astype(jnp.bfloat16)
    hidden_grad = jnp.dot(output_grad, down_weight.T, preferred_element_type=jnp.float32)
    up_pre_grad = (hidden_grad * activated).astype(jnp.bfloat16)
    gate_pre_grad = (hidden_grad * up_float * silu_slope(gate_float)).astype(jnp.bfloat16)
    total = jnp.zeros((FF, D), jnp.float32)
    for source in range(N_ROW):
        lower = source * TOK_ROW
        term = jnp.dot(hidden[lower:lower + TOK_ROW].T, output_grad[lower:lower + TOK_ROW], preferred_element_type=jnp.float32)
        total = total + lax.optimization_barrier(term.astype(jnp.bfloat16)).astype(jnp.float32)
    down_weight_grad = total.astype(jnp.bfloat16)

    windows = N_ROW // 2
    picks = []
    chosen_rows = []
    chosen_cots = []
    for source in range(N_ROW):
        lower = source * TOK_ROW
        picked, weighed = slot_tables(route_ids[lower:lower + TOK_ROW], route_gates[lower:lower + TOK_ROW], windows, CAP)
        rows_in = layer_input[lower:lower + TOK_ROW].astype(jnp.float32)
        rows_out = output_grad[lower:lower + TOK_ROW].astype(jnp.float32)
        chosen_rows.append(jnp.einsum("tec,td->ecd", picked, rows_in, precision=lax.Precision.HIGHEST).astype(jnp.bfloat16))
        scaled = jnp.einsum("tec,td->ecd", picked, rows_out, precision=lax.Precision.HIGHEST) * weighed[:, :, None]
        chosen_cots.append(scaled.astype(jnp.bfloat16))
        picks.append(picked)
    chosen_rows = jnp.stack(chosen_rows)
    chosen_cots = jnp.stack(chosen_cots)

    half = FF // 2
    gate_grads = []
    up_grads = []
    down_grads = []
    returned = []
    for expert in range(windows):
        rows_x = chosen_rows[:, expert].reshape(N_ROW * CAP, D)
        rows_d = chosen_cots[:, expert].reshape(N_ROW * CAP, D)
        weight_gate = jnp.concatenate([expert_gate[2 * expert], expert_gate[2 * expert + 1]], axis=1)
        weight_up = jnp.concatenate([expert_up[2 * expert], expert_up[2 * expert + 1]], axis=1)
        weight_down = jnp.concatenate([expert_down[2 * expert], expert_down[2 * expert + 1]], axis=0)
        gate_value = jnp.dot(rows_x, weight_gate, preferred_element_type=jnp.float32)
        up_value = jnp.dot(rows_x, weight_up, preferred_element_type=jnp.float32)
        active = jax.nn.silu(gate_value)
        inner = (active * up_value).astype(jnp.bfloat16)
        inner_grad = jnp.dot(rows_d, weight_down.T, preferred_element_type=jnp.float32)
        down_full = jnp.dot(inner.T, rows_d, preferred_element_type=jnp.float32).astype(jnp.bfloat16)
        up_local = (inner_grad * active).astype(jnp.bfloat16)
        gate_local = (inner_grad * up_value * silu_slope(gate_value)).astype(jnp.bfloat16)
        gate_full = jnp.dot(rows_x.T, gate_local, preferred_element_type=jnp.float32).astype(jnp.bfloat16)
        up_full = jnp.dot(rows_x.T, up_local, preferred_element_type=jnp.float32).astype(jnp.bfloat16)
        back = jnp.dot(gate_local, weight_gate.T, preferred_element_type=jnp.float32) + jnp.dot(up_local, weight_up.T, preferred_element_type=jnp.float32)
        gate_grads += [gate_full[:, :half], gate_full[:, half:]]
        up_grads += [up_full[:, :half], up_full[:, half:]]
        down_grads += [down_full[:half], down_full[half:]]
        returned.append(back.reshape(N_ROW, CAP, D))
    returned = jnp.stack(returned, axis=1)
    blocks = [jnp.einsum("tec,ecd->td", picks[source], returned[source], precision=lax.Precision.HIGHEST) for source in range(N_ROW)]
    moe_input_grad = jnp.concatenate(blocks, axis=0).astype(jnp.bfloat16)
    return (gate_pre_grad, up_pre_grad, down_weight_grad, jnp.stack(gate_grads), jnp.stack(up_grads), jnp.stack(down_grads), moe_input_grad)
```

```python
import jax
import jax.numpy as jnp
from jax import lax
from jax.experimental import pallas as pl
from jax.experimental.pallas import tpu as pltpu
from jax.sharding import PartitionSpec as P

TOK = 1024
FEAT = 448
PAIR = 2 * FEAT
FFD = 304
HID = 152
ROWS = 8
CHIPS = 8
WIN = 4
CAP = 24
PAD = 32
SLOTS = ROWS * CAP
HALF = SLOTS // 2

F32 = jnp.float32
BF16 = jnp.bfloat16
MESH = pl.DeviceIdType.MESH

NN = (((1,), (0,)), ((), ()))
NT = (((1,), (1,)), ((), ()))
TN = (((0,), (0,)), ((), ()))


def dot(a, b, dims):
    return lax.dot_general(a, b, dims, preferred_element_type=F32)


def slope_of(values, sigma):
    return sigma * (1.0 + values * (1.0 - sigma))


class Channels:
    def __init__(self, send, recv):
        self.send, self.recv, self.used, self.sent = send, recv, 0, []

    def take(self, count=1):
        first = self.used
        self.used += count
        return first

    def copy(self, src, dst, device, index=None):
        index = self.take() if index is None else index
        return pltpu.make_async_remote_copy(
            src_ref=src,
            dst_ref=dst,
            send_sem=self.send.at[index],
            recv_sem=self.recv.at[index],
            device_id=device,
            device_id_type=MESH,
        )

    def go(self, src, dst, device):
        made = self.copy(src, dst, device)
        made.start()
        self.sent.append(made)
        return made


CHANNELS = 128


class RingPair:
    def __init__(self, ch, slot, cut, size, pos, side, right, left, across):
        self.ch, self.slot, self.cut, self.size = ch, slot, cut, size
        self.pos, self.side = pos, side
        self.right, self.left, self.across = right, left, across

    def at(self, delta, flip):
        return self.slot((self.pos + delta) % 4, (self.side + flip) % 2)

    def own(self, src):
        dst = self.at(0, 0)
        self.a = self.ch.go(src, dst, self.right)
        self.b = self.ch.go(src, dst, self.left)
        self.c = self.ch.go(src, dst, self.across)

    def wait_own(self):
        self.a.wait_recv()
        self.b.wait_recv()
        self.c.wait_recv()

    def _far(self, flip):
        lo, hi = pl.ds(0, self.cut), pl.ds(self.cut, self.size - self.cut)
        from_left, from_right = self.at(3, flip), self.at(1, flip)
        return (
            self.ch.go(from_left.at[lo], from_left.at[lo], self.right),
            self.ch.go(from_right.at[hi], from_right.at[hi], self.left),
        )

    def far(self):
        self.d = self._far(0)

    def wait_far(self):
        self.d[0].wait_recv()
        self.d[1].wait_recv()

    def other(self):
        src = self.at(0, 1)
        self.e = (self.ch.go(src, src, self.right), self.ch.go(src, src, self.left))

    def wait_other(self):
        self.e[0].wait_recv()
        self.e[1].wait_recv()

    def other_far(self):
        self.f = self._far(1)

    def wait_other_far(self):
        self.f[0].wait_recv()
        self.f[1].wait_recv()


def kernel(
    ids_ref, gates_ref, gp_ref, up_ref, og, li, dw, wg, wu, wd,
    gpg_ref, upg_ref, dwg_ref, gg, ug, dg, mig_ref,
    panel, li_pair, dw_all, d_send, d_recv, rows, w_gate, w_up, w_down,
    e_part, e_sib, e_sum, e_recv, c_send, c_recv, g_send, f_recv,
    picked, hidden, hg, mids, back, send_sems, recv_sems, local_sems,
):
    r = lax.axis_index("row")
    c = lax.axis_index("col")
    yl, z = r // 4, r % 4
    x, yh, k = c // 4, (c // 2) % 2, c % 2
    chip = c // 2

    def row_of(yl_, z_):
        return yl_ * 4 + z_

    def chip_of(x_, yh_):
        return x_ * 2 + yh_

    def col_dev(x_, yh_):
        return (r, chip_of(x_, yh_) * 2 + k)

    def row_dev(row_):
        return (row_, c)

    sib = (r, chip * 2 + (1 - k))

    barrier = pltpu.get_barrier_semaphore()
    greeted = 0
    for o in range(1, 8):
        pl.semaphore_signal(barrier, inc=1, device_id=row_dev((r + o) % 8), device_id_type=MESH)
        pl.semaphore_signal(
            barrier, inc=1, device_id=col_dev((x + o // 2) % 4, (yh + o % 2) % 2), device_id_type=MESH
        )
        greeted += 2
    for o in range(8):
        pl.semaphore_signal(
            barrier, inc=1, device_id=((r + o) % 8, chip * 2 + (1 - k)), device_id_type=MESH
        )
        greeted += 1
    pl.semaphore_wait(barrier, greeted)

    ch = Channels(send_sems, recv_sems)
    lanes = pl.ds(pl.multiple_of(k * FEAT, FEAT), FEAT)

    def panel_slot(x_, yh_):
        return panel.at[chip_of(x_, yh_), lanes]

    def rows_slot(x_, yh_):
        return rows.at[k, chip_of(x_, yh_)]

    def dw_slot(z_, yl_):
        return dw_all.at[row_of(yl_, z_)]

    x_right, x_left, y_across = col_dev((x + 1) % 4, yh), col_dev((x + 3) % 4, yh), col_dev(x, 1 - yh)
    ga = RingPair(ch, panel_slot, FEAT // 2, FEAT, x, yh, x_right, x_left, y_across)
    gc = RingPair(ch, rows_slot, HALF, SLOTS, x, yh, x_right, x_left, y_across)
    gb = RingPair(
        ch, dw_slot, 160, FFD, z, yl,
        row_dev(row_of(yl, (z + 1) % 4)), row_dev(row_of(yl, (z + 3) % 4)), row_dev(row_of(1 - yl, z)),
    )

    li_slot = li_pair.at[lanes]
    own_slot = panel_slot(x, yh)
    sib_og = ch.go(og, own_slot, sib)
    sib_li = ch.go(li, li_slot, sib)
    ga.own(og)
    gb.own(dw)
    local = [
        pltpu.make_async_copy(og, own_slot, local_sems.at[0]),
        pltpu.make_async_copy(li, li_slot, local_sems.at[1]),
        pltpu.make_async_copy(dw, dw_slot(z, yl), local_sems.at[2]),
        pltpu.make_async_copy(wg, w_gate, local_sems.at[3]),
        pltpu.make_async_copy(wu, w_up, local_sems.at[4]),
        pltpu.make_async_copy(wd, w_down, local_sems.at[5]),
    ]
    for each in local:
        each.start()

    ids0, ids1 = ids_ref[0:1, :], ids_ref[1:2, :]
    expert = lax.broadcasted_iota(jnp.int32, (8, TOK), 0)
    lane = lax.broadcasted_iota(jnp.int32, (8, TOK), 1)
    first = (jnp.broadcast_to(ids0, (8, TOK)) == expert).astype(F32)
    second = (jnp.broadcast_to(ids1, (8, TOK)) == expert).astype(F32)
    hits = first + second
    ranks = hits
    step = 1
    while step < TOK:
        ranks = ranks + jnp.where(lane >= step, pltpu.roll(ranks, step, 1), 0.0)
        step *= 2
    ranks = (ranks - hits).astype(jnp.int32)
    gate_of = first * gates_ref[0:1, :] + second * gates_ref[1:2, :]
    place = lax.broadcasted_iota(jnp.int32, (PAD, TOK), 0)
    weights = []
    for e in range(WIN):
        same = jnp.broadcast_to(ranks[e : e + 1, :], (PAD, TOK)) == place
        mine = jnp.where(same & (place < CAP), jnp.broadcast_to(hits[e : e + 1, :], (PAD, TOK)), 0.0)
        picked[pl.ds(e * PAD, PAD), :] = mine.astype(BF16)
        weights.append(jnp.sum(mine * gate_of[e : e + 1, :], axis=1, keepdims=True))
    weights = jnp.concatenate(weights, axis=0)

    local[0].wait()
    local[1].wait()
    sib_og.wait_recv()
    sib_li.wait_recv()

    @pl.when(k == 0)
    def _():
        chosen = dot(picked[...], li_pair[...], NT)
        c_send[...] = chosen.astype(BF16).reshape(WIN, PAD, PAIR)

    @pl.when(k == 1)
    def _():
        chosen = dot(picked[...], panel[chip], NT) * weights
        c_send[...] = chosen.astype(BF16).reshape(WIN, PAD, PAIR)

    to_experts = []
    for o in range(1, 8):
        dest = (r + o) % 8
        to_experts.append(ch.go(c_send.at[dest // 2], c_recv.at[r], row_dev(dest)))
    keep = pltpu.make_async_copy(c_send.at[r // 2], c_recv.at[r], local_sems.at[6])
    keep.start()

    def hide(i, carry):
        part = pl.ds(pl.multiple_of(i * 16, 16), 16)
        v = gp_ref[part, :].astype(F32)
        hidden[part, :] = (v * jax.nn.sigmoid(v) * up_ref[part, :].astype(F32)).astype(BF16)
        return carry

    lax.fori_loop(0, FFD // 16, hide, 0)

    for each in to_experts:
        each.wait_recv()
    keep.wait()
    packed = c_recv[...].astype(F32)[:, :CAP, :].reshape(SLOTS, PAIR).astype(BF16)
    rows[k, chip] = packed
    gc_own = gc.at(0, 0)
    c_sib = {(0, 0): ch.go(gc_own, gc_own, sib)}
    gc.own(gc_own)

    d_first = ch.take(8)

    def down_block(o):
        j = chip_of((x + o // 2) % 4, (yh + o % 2) % 2)
        d_send[j] = dot(hidden[...], panel[j], NT).astype(BF16)

        @pl.when(j != r)
        def _():
            down_copy(j).start()

    def down_copy(j):
        return pltpu.make_async_remote_copy(
            src_ref=d_send.at[j],
            dst_ref=d_recv.at[r],
            send_sem=send_sems.at[d_first + j],
            recv_sem=recv_sems.at[d_first + r],
            device_id=row_dev(j),
            device_id_type=MESH,
        )

    def forward(gather, kept, offsets):
        for o in offsets:
            slot = gather.at(o // 2, o % 2)
            kept[(o // 2, o % 2)] = ch.go(slot, slot, sib)

    down_block(0)

    a_sib = {}
    ga.wait_own()
    forward(ga, a_sib, (1, 2, 6))
    ga.far()
    gb.wait_own()
    gb.far()
    gb.other()

    gc.wait_own()
    gc.other()
    gc.far()
    forward(gc, c_sib, (1, 2, 6))

    for o in (1, 2, 6):
        a_sib[(o // 2, o % 2)].wait_recv()

    def near(i, carry):
        down_block(jnp.where(i == 0, 1, jnp.where(i == 1, 2, 6)))
        return carry

    lax.fori_loop(0, 3, near, 0)

    gc.wait_other()
    gc.other_far()
    gc.wait_far()
    forward(gc, c_sib, (3, 4, 7))
    ga.wait_far()
    forward(ga, a_sib, (4,))
    ga.other()
    gb.wait_other()
    gb.other_far()
    gb.wait_far()
    gc.wait_other_far()
    forward(gc, c_sib, (5,))
    a_sib[(2, 0)].wait_recv()
    down_block(4)
    for each in c_sib.values():
        each.wait_recv()
    for each in local[3:]:
        each.wait()

    mids[...] = jnp.zeros_like(mids)

    def lanes_of(i):
        return pl.ds(pl.multiple_of(i * PAIR, 128), PAIR)

    def enter(i, carry):
        part = lanes_of(i)
        taken = rows[0, i]
        mids[0] += dot(taken, w_gate[:, part], NT)
        mids[1] += dot(taken, w_up[:, part], NT)
        mids[2] += dot(rows[1, i], w_down[:, part], NT)
        return carry

    lax.fori_loop(0, CHIPS, enter, 0)
    gate_value, up_value, inner_grad = mids[0], mids[1], mids[2]
    sigma = jax.nn.sigmoid(gate_value)
    active = gate_value * sigma
    inner = (active * up_value).astype(BF16)
    up_local = (inner_grad * active).astype(BF16)
    gate_local = (inner_grad * up_value * slope_of(gate_value, sigma)).astype(BF16)

    def leave(i, carry):
        part = lanes_of(i)
        total = dot(gate_local, w_gate[:, part], NN) + dot(up_local, w_up[:, part], NN)
        e_part[i] = total.astype(BF16)
        return carry

    lax.fori_loop(0, CHIPS, leave, 0)

    mine = pl.ds(pl.multiple_of(k * HALF, HALF), HALF)
    theirs = pl.ds(pl.multiple_of((1 - k) * HALF, HALF), HALF)
    between = ch.go(e_part.at[:, theirs], e_sib, sib)

    ga.wait_other()
    ga.other_far()
    forward(ga, a_sib, (3, 7))
    between.wait_recv()

    def add_sib(i, carry):
        e_sum[i] = (e_part[i, mine].astype(F32) + e_sib[i].astype(F32)).astype(BF16)
        return carry

    lax.fori_loop(0, CHIPS, add_sib, 0)
    to_chips = []
    for o in range(1, 8):
        x_, yh_ = (x + o // 2) % 4, (yh + o % 2) % 2
        to_chips.append(ch.go(e_sum.at[chip_of(x_, yh_)], e_recv.at[o], col_dev(x_, yh_)))

    def grads(i, carry):
        part = lanes_of(i)
        taken = rows[0, i]
        w_gate[:, part] = dot(gate_local, taken, TN).astype(BF16)
        w_up[:, part] = dot(up_local, taken, TN).astype(BF16)
        w_down[:, part] = dot(inner, rows[1, i], TN).astype(BF16)
        return carry

    lax.fori_loop(0, CHIPS, grads, 0)
    stores = [
        pltpu.make_async_copy(w_gate, gg, local_sems.at[7]),
        pltpu.make_async_copy(w_up, ug, local_sems.at[8]),
        pltpu.make_async_copy(w_down, dg, local_sems.at[9]),
    ]
    for each in stores:
        each.start()

    a_sib[(1, 1)].wait_recv()
    a_sib[(3, 1)].wait_recv()

    def partner(i, carry):
        down_block(jnp.where(i == 0, 3, 7))
        return carry

    lax.fori_loop(0, 2, partner, 0)

    gb.wait_other_far()
    local[2].wait()

    def hidden_block(o):
        j = chip_of((x + o // 2) % 4, (yh + o % 2) % 2)
        return dot(dw_all[j], panel[j], NN)

    hg[...] = hidden_block(0)

    def accumulate(i, carry):
        hg[...] += hidden_block(jnp.where(i < 5, i, i + 1))
        return carry

    lax.fori_loop(1, 7, accumulate, 0)

    ga.wait_other_far()
    forward(ga, a_sib, (5,))
    for each in to_chips:
        each.wait_recv()
    returned = e_sum[chip].astype(F32)
    for o in range(1, 8):
        returned = returned + e_recv[o].astype(F32)
    returned = returned.reshape(ROWS // 2, CAP, PAIR)
    filled = jnp.concatenate([returned, jnp.zeros((ROWS // 2, PAD - CAP, PAIR), F32)], axis=1)
    g_send[...] = filled.astype(BF16)

    home_first = ch.take(8)
    home_send = ch.take(8)

    def home_copy(i, core):
        dest = (k * 4 + i, chip * 2 + core)
        return pltpu.make_async_remote_copy(
            src_ref=g_send.at[i],
            dst_ref=f_recv.at[r],
            send_sem=send_sems.at[home_send + i * 2 + core],
            recv_sem=recv_sems.at[home_first + r],
            device_id=dest,
            device_id_type=MESH,
        )

    def home_self(i, core):
        return (k * 4 + i == r) & (core == k)

    for i in range(4):
        for core in range(2):
            @pl.when(jnp.logical_not(home_self(i, core)))
            def _(i=i, core=core):
                home_copy(i, core).start()

    @pl.when(r // 4 == k)
    def _():
        f_recv[r] = g_send[r % 4]

    a_sib[(2, 1)].wait_recv()
    down_block(5)
    hg[...] += hidden_block(5)

    def finish(i, carry):
        part = pl.ds(pl.multiple_of(i * 16, 16), 16)
        v = gp_ref[part, :].astype(F32)
        sigma = jax.nn.sigmoid(v)
        grad = hg[part, :]
        upg_ref[part, :] = (grad * (v * sigma)).astype(BF16)
        gpg_ref[part, :] = (grad * up_ref[part, :].astype(F32) * slope_of(v, sigma)).astype(BF16)
        return carry

    lax.fori_loop(0, FFD // 16, finish, 0)

    def home_arrival(source):
        return pltpu.make_async_remote_copy(
            src_ref=g_send.at[0],
            dst_ref=f_recv.at[source],
            send_sem=send_sems.at[home_send],
            recv_sem=recv_sems.at[home_first + source],
            device_id=sib,
            device_id_type=MESH,
        )

    for o in range(1, 8):
        home_arrival((r + o) % 8).wait_recv()

    @pl.when(r // 4 != k)
    def _():
        home_arrival(r).wait_recv()

    halves = f_recv[...].astype(F32).reshape(WIN, 2, PAD, PAIR)
    combined = (halves[:, 0] + halves[:, 1]).reshape(WIN * PAD, PAIR)
    back[...] = jnp.transpose(combined).astype(BF16)
    mig_ref[...] = dot(back[lanes, :], picked[...], NN).astype(BF16)

    def down_arrival(source):
        return pltpu.make_async_remote_copy(
            src_ref=d_send.at[0],
            dst_ref=d_recv.at[source],
            send_sem=send_sems.at[d_first],
            recv_sem=recv_sems.at[d_first + source],
            device_id=sib,
            device_id_type=MESH,
        )

    for o in range(1, 8):
        down_arrival((r + o) % 8).wait_recv()

    def add_down(i, carry):
        part = pl.ds(pl.multiple_of(i * 16, 16), 16)
        total = d_send[r, part].astype(F32)
        for o in range(1, 8):
            total = total + d_recv[(r + o) % 8, part].astype(F32)
        dwg_ref[part, :] = total.astype(BF16)
        return carry

    lax.fori_loop(0, FFD // 16, add_down, 0)

    for each in stores:
        each.wait()
    for each in ch.sent:
        each.wait_send()
    for j in range(8):
        @pl.when(j != r)
        def _(j=j):
            down_copy(j).wait_send()
    for i in range(4):
        for core in range(2):
            @pl.when(jnp.logical_not(home_self(i, core)))
            def _(i=i, core=core):
                home_copy(i, core).wait_send()


def body(
    layer_input, output_grad, gate_pre, up_pre, down_weight,
    route_ids, route_gates, expert_gate, expert_up, expert_down,
):
    vmem = pl.BlockSpec(memory_space=pltpu.VMEM)
    hbm = pl.BlockSpec(memory_space=pl.ANY)

    def shape(*dims, dtype=BF16):
        return jax.ShapeDtypeStruct(dims, dtype)

    def scratch(*dims, dtype=BF16):
        return pltpu.VMEM(dims, dtype)

    outs = pl.pallas_call(
        kernel,
        out_shape=(
            shape(FFD, TOK), shape(FFD, TOK), shape(FFD, PAIR),
            shape(HID, CHIPS * PAIR), shape(HID, CHIPS * PAIR), shape(HID, CHIPS * PAIR),
            shape(FEAT, TOK),
        ),
        in_specs=[vmem] * 4 + [hbm] * 6,
        out_specs=(vmem, vmem, vmem, hbm, hbm, hbm, vmem),
        scratch_shapes=[
            scratch(CHIPS, PAIR, TOK),
            scratch(PAIR, TOK),
            scratch(ROWS, FFD, PAIR),
            scratch(ROWS, FFD, PAIR),
            scratch(ROWS, FFD, PAIR),
            scratch(2, CHIPS, SLOTS, PAIR),
            scratch(HID, CHIPS * PAIR),
            scratch(HID, CHIPS * PAIR),
            scratch(HID, CHIPS * PAIR),
            scratch(CHIPS, SLOTS, PAIR),
            scratch(CHIPS, HALF, PAIR),
            scratch(CHIPS, HALF, PAIR),
            scratch(CHIPS, HALF, PAIR),
            scratch(WIN, PAD, PAIR),
            scratch(ROWS, PAD, PAIR),
            scratch(ROWS // 2, PAD, PAIR),
            scratch(ROWS, PAD, PAIR),
            scratch(WIN * PAD, TOK),
            scratch(FFD, TOK),
            scratch(FFD, TOK, dtype=F32),
            scratch(3, SLOTS, HID, dtype=F32),
            scratch(PAIR, WIN * PAD),
            pltpu.SemaphoreType.DMA((CHANNELS,)),
            pltpu.SemaphoreType.DMA((CHANNELS,)),
            pltpu.SemaphoreType.DMA((16,)),
        ],
        compiler_params=pltpu.CompilerParams(
            collective_id=0, has_side_effects=True, vmem_limit_bytes=63 * 1024 * 1024
        ),
        name="layer_backward",
    )(
        route_ids.T, route_gates.T, gate_pre.T, up_pre.T, output_grad.T, layer_input.T, down_weight,
        expert_gate[0].T, expert_up[0].T, expert_down[0],
    )
    gpg, upg, dwg, gg, ug, dg, mig = outs
    return gpg.T, upg.T, dwg, gg.T[None], ug.T[None], dg[None], mig.T


def solution(mesh):
    in_specs = (
        P("row", "col"),
        P("row", "col"),
        P("row", "col"),
        P("row", "col"),
        P("col", "row"),
        P("row", None),
        P("row", None),
        P("row", None, "col"),
        P("row", None, "col"),
        P("row", "col", None),
    )
    out_specs = (
        P("row", "col"),
        P("row", "col"),
        P("col", "row"),
        P("row", None, "col"),
        P("row", None, "col"),
        P("row", "col", None),
        P("row", "col"),
    )
    return jax.shard_map(body, mesh=mesh, in_specs=in_specs, out_specs=out_specs, check_vma=False)
```

```python
import jax
import jax.numpy as jnp
from jax import lax
from jax.experimental import pallas as pl
from jax.experimental.pallas import tpu as pltpu
from jax.sharding import PartitionSpec as P

TOK = 1024
FEAT = 448
PAIR = 2 * FEAT
FFD = 304
HID = 152
ROWS = 8
CHIPS = 8
WIN = 4
CAP = 24
PAD = 32
SLOTS = ROWS * CAP
HALF = SLOTS // 2

F32 = jnp.float32
BF16 = jnp.bfloat16
MESH = pl.DeviceIdType.MESH

NN = (((1,), (0,)), ((), ()))
NT = (((1,), (1,)), ((), ()))
TN = (((0,), (0,)), ((), ()))


def dot(a, b, dims):
    return lax.dot_general(a, b, dims, preferred_element_type=F32)


def slope_of(values, sigma):
    return sigma * (1.0 + values * (1.0 - sigma))


class Channels:
    def __init__(self, send, recv):
        self.send, self.recv, self.used, self.sent = send, recv, 0, []

    def take(self, count=1):
        first = self.used
        self.used += count
        return first

    def copy(self, src, dst, device, index=None):
        index = self.take() if index is None else index
        return pltpu.make_async_remote_copy(
            src_ref=src,
            dst_ref=dst,
            send_sem=self.send.at[index],
            recv_sem=self.recv.at[index],
            device_id=device,
            device_id_type=MESH,
        )

    def go(self, src, dst, device):
        made = self.copy(src, dst, device)
        made.start()
        self.sent.append(made)
        return made


CHANNELS = 128


class RingPair:
    def __init__(self, ch, slot, cut, size, pos, side, right, left, across):
        self.ch, self.slot, self.cut, self.size = ch, slot, cut, size
        self.pos, self.side = pos, side
        self.right, self.left, self.across = right, left, across

    def at(self, delta, flip):
        return self.slot((self.pos + delta) % 4, (self.side + flip) % 2)

    def own_near(self, src):
        dst = self.at(0, 0)
        self.a = self.ch.go(src, dst, self.right)
        self.b = self.ch.go(src, dst, self.left)

    def own_across(self, src):
        self.c = self.ch.go(src, self.at(0, 0), self.across)

    def _far(self, flip):
        lo, hi = pl.ds(0, self.cut), pl.ds(self.cut, self.size - self.cut)
        from_left, from_right = self.at(3, flip), self.at(1, flip)
        return (
            self.ch.go(from_left.at[lo], from_left.at[lo], self.right),
            self.ch.go(from_right.at[hi], from_right.at[hi], self.left),
        )

    def near_done(self):
        self.a.wait_recv()
        self.b.wait_recv()

    def far(self):
        self.d = self._far(0)

    def across_done(self):
        self.c.wait_recv()
        src = self.at(0, 1)
        self.e = (self.ch.go(src, src, self.right), self.ch.go(src, src, self.left))

    def far_done(self):
        for each in self.d:
            each.wait_recv()

    def other_done(self):
        for each in self.e:
            each.wait_recv()
        self.f = self._far(1)

    def all_done(self):
        for each in self.f:
            each.wait_recv()


def kernel(
    ids_ref, gates_ref, gp_ref, up_ref, og, li, dw, wg, wu, wd,
    gpg_ref, upg_ref, dwg_ref, gg, ug, dg, mig_ref,
    panel, li_pair, dw_all, d_send, y_recv, z_recv, rows, w_gate, w_up, w_down,
    e_part, e_sib, e_sum, e_recv, c_send, c_recv, g_send, f_recv,
    picked, hidden, hg, mids, back, send_sems, recv_sems, local_sems,
):
    r = lax.axis_index("row")
    c = lax.axis_index("col")
    yl, z = r // 4, r % 4
    x, yh, k = c // 4, (c // 2) % 2, c % 2
    chip = c // 2

    def row_of(yl_, z_):
        return yl_ * 4 + z_

    def chip_of(x_, yh_):
        return x_ * 2 + yh_

    def col_dev(x_, yh_):
        return (r, chip_of(x_, yh_) * 2 + k)

    def row_dev(row_):
        return (row_, c)

    sib = (r, chip * 2 + (1 - k))

    barrier = pltpu.get_barrier_semaphore()
    greeted = 0
    for o in range(1, 8):
        pl.semaphore_signal(barrier, inc=1, device_id=row_dev((r + o) % 8), device_id_type=MESH)
        pl.semaphore_signal(
            barrier, inc=1, device_id=col_dev((x + o // 2) % 4, (yh + o % 2) % 2), device_id_type=MESH
        )
        greeted += 2
    for o in range(8):
        pl.semaphore_signal(
            barrier, inc=1, device_id=((r + o) % 8, chip * 2 + (1 - k)), device_id_type=MESH
        )
        greeted += 1
    pl.semaphore_wait(barrier, greeted)

    ch = Channels(send_sems, recv_sems)
    lanes = pl.ds(pl.multiple_of(k * FEAT, FEAT), FEAT)

    def panel_slot(x_, yh_):
        return panel.at[chip_of(x_, yh_), lanes]

    def rows_slot(x_, yh_):
        return rows.at[k, chip_of(x_, yh_)]

    def dw_slot(z_, yl_):
        return dw_all.at[row_of(yl_, z_)]

    x_right, x_left, y_across = col_dev((x + 1) % 4, yh), col_dev((x + 3) % 4, yh), col_dev(x, 1 - yh)
    ga = RingPair(ch, panel_slot, FEAT // 2, FEAT, x, yh, x_right, x_left, y_across)
    gc = RingPair(ch, rows_slot, HALF, SLOTS, x, yh, x_right, x_left, y_across)
    gb = RingPair(
        ch, dw_slot, 160, FFD, z, yl,
        row_dev(row_of(yl, (z + 1) % 4)), row_dev(row_of(yl, (z + 3) % 4)), row_dev(row_of(1 - yl, z)),
    )

    li_slot = li_pair.at[lanes]
    own_slot = panel_slot(x, yh)
    sib_og = ch.go(og, own_slot, sib)
    sib_li = ch.go(li, li_slot, sib)
    ga.own_near(og)
    ga.own_across(og)
    local = [
        pltpu.make_async_copy(og, own_slot, local_sems.at[0]),
        pltpu.make_async_copy(li, li_slot, local_sems.at[1]),
        pltpu.make_async_copy(dw, dw_slot(z, yl), local_sems.at[2]),
        pltpu.make_async_copy(wg, w_gate, local_sems.at[3]),
        pltpu.make_async_copy(wu, w_up, local_sems.at[4]),
        pltpu.make_async_copy(wd, w_down, local_sems.at[5]),
    ]
    for each in local:
        each.start()

    ids0, ids1 = ids_ref[0:1, :], ids_ref[1:2, :]
    expert = lax.broadcasted_iota(jnp.int32, (8, TOK), 0)
    lane = lax.broadcasted_iota(jnp.int32, (8, TOK), 1)
    first = (jnp.broadcast_to(ids0, (8, TOK)) == expert).astype(F32)
    second = (jnp.broadcast_to(ids1, (8, TOK)) == expert).astype(F32)
    hits = first + second
    ranks = hits
    step = 1
    while step < TOK:
        ranks = ranks + jnp.where(lane >= step, pltpu.roll(ranks, step, 1), 0.0)
        step *= 2
    ranks = (ranks - hits).astype(jnp.int32)
    gate_of = first * gates_ref[0:1, :] + second * gates_ref[1:2, :]
    place = lax.broadcasted_iota(jnp.int32, (PAD, TOK), 0)
    weights = []
    for e in range(WIN):
        same = jnp.broadcast_to(ranks[e : e + 1, :], (PAD, TOK)) == place
        mine = jnp.where(same & (place < CAP), jnp.broadcast_to(hits[e : e + 1, :], (PAD, TOK)), 0.0)
        picked[pl.ds(e * PAD, PAD), :] = mine.astype(BF16)
        weights.append(jnp.sum(mine * gate_of[e : e + 1, :], axis=1, keepdims=True))
    weights = jnp.concatenate(weights, axis=0)

    local[0].wait()
    local[1].wait()
    sib_og.wait_recv()
    sib_li.wait_recv()

    @pl.when(k == 0)
    def _():
        chosen = dot(picked[...], li_pair[...], NT)
        c_send[...] = chosen.astype(BF16).reshape(WIN, PAD, PAIR)

    @pl.when(k == 1)
    def _():
        chosen = dot(picked[...], panel[chip], NT) * weights
        c_send[...] = chosen.astype(BF16).reshape(WIN, PAD, PAIR)

    to_experts = []
    for o in range(1, 8):
        dest = (r + o) % 8
        to_experts.append(ch.go(c_send.at[dest // 2], c_recv.at[r], row_dev(dest)))
    keep = pltpu.make_async_copy(c_send.at[r // 2], c_recv.at[r], local_sems.at[6])
    keep.start()

    gb.own_near(dw)

    def hide(i, carry):
        part = pl.ds(pl.multiple_of(i * 16, 16), 16)
        v = gp_ref[part, :].astype(F32)
        hidden[part, :] = (v * jax.nn.sigmoid(v) * up_ref[part, :].astype(F32)).astype(BF16)
        return carry

    lax.fori_loop(0, FFD // 16, hide, 0)

    y_first = ch.take(4)
    y_out = ch.take(8)
    z_first = ch.take(4)
    z_out = ch.take(4)

    def chip_at(o):
        return chip_of((x + o // 2) % 4, (yh + o % 2) % 2)

    def y_copy(j):
        return pltpu.make_async_remote_copy(
            src_ref=d_send.at[j],
            dst_ref=y_recv.at[j % 4],
            send_sem=send_sems.at[y_out + j],
            recv_sem=recv_sems.at[y_first + j % 4],
            device_id=row_dev(row_of(1 - yl, z)),
            device_id_type=MESH,
        )

    def z_copy(to):
        return pltpu.make_async_remote_copy(
            src_ref=d_send.at[row_of(yl, to)],
            dst_ref=z_recv.at[z],
            send_sem=send_sems.at[z_out + to],
            recv_sem=recv_sems.at[z_first + z],
            device_id=row_dev(row_of(yl, to)),
            device_id_type=MESH,
        )

    def z_arrival(source):
        return pltpu.make_async_remote_copy(
            src_ref=d_send.at[0],
            dst_ref=z_recv.at[source],
            send_sem=send_sems.at[z_out],
            recv_sem=recv_sems.at[z_first + source],
            device_id=sib,
            device_id_type=MESH,
        )

    def down_block(o):
        j = chip_at(o)
        d_send[j] = dot(hidden[...], panel[j], NT).astype(BF16)

        @pl.when(j // 4 != yl)
        def _():
            y_copy(j).start()

    def down_join(o):
        j = chip_at(o)
        to = j % 4

        @pl.when(j // 4 == yl)
        def _():
            y_copy(j).wait_recv()

            def add(i, carry):
                part = pl.ds(pl.multiple_of(i * 16, 16), 16)
                d_send[j, part] = (d_send[j, part].astype(F32) + y_recv[to, part].astype(F32)).astype(BF16)
                return carry

            lax.fori_loop(0, FFD // 16, add, 0)

            @pl.when(to != z)
            def _():
                z_copy(to).start()


    for each in to_experts:
        each.wait_recv()
    keep.wait()
    packed = c_recv[...].astype(F32)[:, :CAP, :].reshape(SLOTS, PAIR).astype(BF16)
    rows[k, chip] = packed
    gc_own = gc.at(0, 0)
    c_sib = {0: ch.go(gc_own, gc_own, sib)}
    gc.own_near(gc_own)
    gc.own_across(gc_own)

    def forward(gather, kept, offsets):
        for o in offsets:
            slot = gather.at(o // 2, o % 2)
            kept[o] = ch.go(slot, slot, sib)

    def lanes_of(i):
        return pl.ds(pl.multiple_of(i * PAIR, 128), PAIR)

    def enter(o):
        i = chip_at(o)
        part = lanes_of(i)
        taken = rows[0, i]
        mids[0] += dot(taken, w_gate[:, part], NT)
        mids[1] += dot(taken, w_up[:, part], NT)
        mids[2] += dot(rows[1, i], w_down[:, part], NT)

    def hidden_block(o):
        j = chip_at(o)
        hg[...] += dot(dw_all[j], panel[j], NN)

    def near_offset(i):
        return jnp.where(i == 0, 1, jnp.where(i == 1, 2, 6))

    def over(count, what, offset):
        def step(i, carry):
            what(offset(i))
            return carry

        lax.fori_loop(0, count, step, 0)

    mids[...] = jnp.zeros_like(mids)
    hg[...] = jnp.zeros_like(hg)

    a_sib = {}
    for each in local[3:]:
        each.wait()
    c_sib[0].wait_recv()
    enter(0)
    ga.near_done()
    forward(ga, a_sib, (2, 6))
    ga.far()
    ga.across_done()
    forward(ga, a_sib, (1,))
    gb.own_across(dw)
    down_block(0)
    for o in (1, 2, 6):
        a_sib[o].wait_recv()
    over(3, down_block, near_offset)
    gb.near_done()
    gb.far()
    gc.near_done()
    forward(gc, c_sib, (2, 6))
    gc.across_done()
    gc.far()
    forward(gc, c_sib, (1,))
    for o in (1, 2, 6):
        c_sib[o].wait_recv()
    over(3, enter, near_offset)
    gb.across_done()
    down_join(0)
    over(3, down_join, near_offset)

    ga.far_done()
    forward(ga, a_sib, (4,))
    a_sib[4].wait_recv()
    down_block(4)
    gc.far_done()
    forward(gc, c_sib, (4,))
    gb.far_done()
    gb.other_done()
    c_sib[4].wait_recv()
    enter(4)
    ga.other_done()
    forward(ga, a_sib, (3, 7))
    gc.other_done()
    forward(gc, c_sib, (3, 7))
    for o in (3, 7):
        a_sib[o].wait_recv()
    over(2, down_block, lambda i: 3 + 4 * i)
    down_join(4)
    for o in (3, 7):
        c_sib[o].wait_recv()
    over(2, enter, lambda i: 3 + 4 * i)

    ga.all_done()
    forward(ga, a_sib, (5,))
    a_sib[5].wait_recv()
    down_block(5)
    over(2, down_join, lambda i: 3 + 4 * i)
    gb.all_done()
    local[2].wait()
    over(4, hidden_block, lambda i: i)
    gc.all_done()
    forward(gc, c_sib, (5,))
    c_sib[5].wait_recv()
    enter(5)

    gate_value, up_value, inner_grad = mids[0], mids[1], mids[2]
    sigma = jax.nn.sigmoid(gate_value)
    active = gate_value * sigma
    inner = (active * up_value).astype(BF16)
    up_local = (inner_grad * active).astype(BF16)
    gate_local = (inner_grad * up_value * slope_of(gate_value, sigma)).astype(BF16)

    mine = pl.ds(pl.multiple_of(k * HALF, HALF), HALF)
    theirs = pl.ds(pl.multiple_of((1 - k) * HALF, HALF), HALF)
    between = ch.take(8)
    outward = ch.take(8)

    def to_sib(o):
        return ch.copy(e_part.at[chip_at(o), theirs], e_sib.at[o], sib, between + o)

    def to_chip(o):
        x_, yh_ = (x + o // 2) % 4, (yh + o % 2) % 2
        return ch.copy(e_sum.at[o], e_recv.at[o], col_dev(x_, yh_), outward + o)

    def leave(o):
        i = chip_at(o)
        part = lanes_of(i)
        total = dot(gate_local, w_gate[:, part], NN) + dot(up_local, w_up[:, part], NN)
        e_part[i] = total.astype(BF16)
        to_sib(o).start()

    def join(o):
        to_sib(o).wait_recv()
        e_sum[o] = (e_part[chip_at(o), mine].astype(F32) + e_sib[o].astype(F32)).astype(BF16)

    def part_out(i, carry):
        leave((i + 1) % 8)
        join(i)
        to_chip(i).start()
        return carry

    leave(1)
    lax.fori_loop(1, 8, part_out, 0)
    join(0)

    def grads(i, carry):
        part = lanes_of(i)
        taken = rows[0, i]
        w_gate[:, part] = dot(gate_local, taken, TN).astype(BF16)
        w_up[:, part] = dot(up_local, taken, TN).astype(BF16)
        w_down[:, part] = dot(inner, rows[1, i], TN).astype(BF16)
        return carry

    down_join(5)
    lax.fori_loop(0, CHIPS, grads, 0)
    stores = [
        pltpu.make_async_copy(w_gate, gg, local_sems.at[7]),
        pltpu.make_async_copy(w_up, ug, local_sems.at[8]),
        pltpu.make_async_copy(w_down, dg, local_sems.at[9]),
    ]
    for each in stores:
        each.start()

    over(4, hidden_block, lambda i: 4 + i)

    for o in range(1, 8):
        to_chip(o).wait_recv()
    returned = e_sum[0].astype(F32)
    for o in range(1, 8):
        returned = returned + e_recv[o].astype(F32)
    returned = returned.reshape(ROWS // 2, CAP, PAIR)
    filled = jnp.concatenate([returned, jnp.zeros((ROWS // 2, PAD - CAP, PAIR), F32)], axis=1)
    g_send[...] = filled.astype(BF16)

    home_first = ch.take(8)
    home_send = ch.take(8)

    def home_copy(i, core):
        dest = (k * 4 + i, chip * 2 + core)
        return pltpu.make_async_remote_copy(
            src_ref=g_send.at[i],
            dst_ref=f_recv.at[r],
            send_sem=send_sems.at[home_send + i * 2 + core],
            recv_sem=recv_sems.at[home_first + r],
            device_id=dest,
            device_id_type=MESH,
        )

    def home_self(i, core):
        return (k * 4 + i == r) & (core == k)

    for i in range(4):
        for core in range(2):
            @pl.when(jnp.logical_not(home_self(i, core)))
            def _(i=i, core=core):
                home_copy(i, core).start()

    @pl.when(r // 4 == k)
    def _():
        f_recv[r] = g_send[r % 4]

    def finish(i, carry):
        part = pl.ds(pl.multiple_of(i * 16, 16), 16)
        v = gp_ref[part, :].astype(F32)
        sigma = jax.nn.sigmoid(v)
        grad = hg[part, :]
        upg_ref[part, :] = (grad * (v * sigma)).astype(BF16)
        gpg_ref[part, :] = (grad * up_ref[part, :].astype(F32) * slope_of(v, sigma)).astype(BF16)
        return carry

    lax.fori_loop(0, FFD // 16, finish, 0)

    def home_arrival(source):
        return pltpu.make_async_remote_copy(
            src_ref=g_send.at[0],
            dst_ref=f_recv.at[source],
            send_sem=send_sems.at[home_send],
            recv_sem=recv_sems.at[home_first + source],
            device_id=sib,
            device_id_type=MESH,
        )

    for o in range(1, 8):
        home_arrival((r + o) % 8).wait_recv()

    @pl.when(r // 4 != k)
    def _():
        home_arrival(r).wait_recv()

    halves = f_recv[...].astype(F32).reshape(WIN, 2, PAD, PAIR)
    combined = (halves[:, 0] + halves[:, 1]).reshape(WIN * PAD, PAIR)
    back[...] = jnp.transpose(combined).astype(BF16)
    mig_ref[...] = dot(back[lanes, :], picked[...], NN).astype(BF16)

    for o in range(1, 4):
        z_arrival((z + o) % 4).wait_recv()

    def add_down(i, carry):
        part = pl.ds(pl.multiple_of(i * 16, 16), 16)
        total = d_send[r, part].astype(F32)
        for o in range(1, 4):
            total = total + z_recv[(z + o) % 4, part].astype(F32)
        dwg_ref[part, :] = total.astype(BF16)
        return carry

    lax.fori_loop(0, FFD // 16, add_down, 0)

    for each in stores:
        each.wait()
    for each in ch.sent:
        each.wait_send()
    for o in range(8):
        to_sib(o).wait_send()
        if o:
            to_chip(o).wait_send()
    for j in range(8):
        @pl.when(j // 4 != yl)
        def _(j=j):
            y_copy(j).wait_send()
    for to in range(4):
        @pl.when(to != z)
        def _(to=to):
            z_copy(to).wait_send()
    for i in range(4):
        for core in range(2):
            @pl.when(jnp.logical_not(home_self(i, core)))
            def _(i=i, core=core):
                home_copy(i, core).wait_send()


def pieces(shape):
    width = shape[1] // 2 if shape[1] > 2 * TOK else shape[1]
    return [pl.ds(at, width) for at in range(0, shape[1], width)]


def place_kernel(*refs):
    count = (len(refs) - 2) // 3
    read_sems, write_sems = refs[-2:]
    pairs = []
    for src, dst, held in zip(refs[:count], refs[count : 2 * count], refs[2 * count : 3 * count]):
        for part in pieces(src.shape):
            n = len(pairs)
            pairs.append((
                pltpu.make_async_copy(src.at[:, part], held.at[:, part], read_sems.at[n]),
                pltpu.make_async_copy(held.at[:, part], dst.at[:, part], write_sems.at[n]),
            ))
    for read, _ in pairs:
        read.start()
    for read, write in pairs:
        read.wait()
        write.start()
    for _, write in pairs:
        write.wait()


def place(arrays):
    hbm = pl.BlockSpec(memory_space=pl.ANY)
    count = len(arrays)
    total = sum(len(pieces(a.shape)) for a in arrays)
    return pl.pallas_call(
        place_kernel,
        out_shape=tuple(jax.ShapeDtypeStruct(a.shape, a.dtype) for a in arrays),
        in_specs=[hbm] * count,
        out_specs=(hbm,) * count,
        scratch_shapes=[pltpu.VMEM(a.shape, a.dtype) for a in arrays]
        + [pltpu.SemaphoreType.DMA((total,)), pltpu.SemaphoreType.DMA((total,))],
        compiler_params=pltpu.CompilerParams(vmem_limit_bytes=63 * 1024 * 1024),
        name="place_results",
    )(*arrays)


def body(
    layer_input, output_grad, gate_pre, up_pre, down_weight,
    route_ids, route_gates, expert_gate, expert_up, expert_down,
):
    vmem = pl.BlockSpec(memory_space=pltpu.VMEM)
    hbm = pl.BlockSpec(memory_space=pl.ANY)

    def shape(*dims, dtype=BF16):
        return jax.ShapeDtypeStruct(dims, dtype)

    def scratch(*dims, dtype=BF16):
        return pltpu.VMEM(dims, dtype)

    outs = pl.pallas_call(
        kernel,
        out_shape=(
            shape(FFD, TOK), shape(FFD, TOK), shape(FFD, PAIR),
            shape(HID, CHIPS * PAIR), shape(HID, CHIPS * PAIR), shape(HID, CHIPS * PAIR),
            shape(FEAT, TOK),
        ),
        in_specs=[vmem] * 4 + [hbm] * 6,
        out_specs=(vmem, vmem, vmem, hbm, hbm, hbm, vmem),
        scratch_shapes=[
            scratch(CHIPS, PAIR, TOK),
            scratch(PAIR, TOK),
            scratch(ROWS, FFD, PAIR),
            scratch(ROWS, FFD, PAIR),
            scratch(ROWS // 2, FFD, PAIR),
            scratch(ROWS // 2, FFD, PAIR),
            scratch(2, CHIPS, SLOTS, PAIR),
            scratch(HID, CHIPS * PAIR),
            scratch(HID, CHIPS * PAIR),
            scratch(HID, CHIPS * PAIR),
            scratch(CHIPS, SLOTS, PAIR),
            scratch(CHIPS, HALF, PAIR),
            scratch(CHIPS, HALF, PAIR),
            scratch(CHIPS, HALF, PAIR),
            scratch(WIN, PAD, PAIR),
            scratch(ROWS, PAD, PAIR),
            scratch(ROWS // 2, PAD, PAIR),
            scratch(ROWS, PAD, PAIR),
            scratch(WIN * PAD, TOK),
            scratch(FFD, TOK),
            scratch(FFD, TOK, dtype=F32),
            scratch(3, SLOTS, HID, dtype=F32),
            scratch(PAIR, WIN * PAD),
            pltpu.SemaphoreType.DMA((CHANNELS,)),
            pltpu.SemaphoreType.DMA((CHANNELS,)),
            pltpu.SemaphoreType.DMA((16,)),
        ],
        compiler_params=pltpu.CompilerParams(
            collective_id=0, has_side_effects=True, vmem_limit_bytes=63 * 1024 * 1024
        ),
        name="layer_backward",
    )(
        route_ids.T, route_gates.T, gate_pre.T, up_pre.T, output_grad.T, layer_input.T, down_weight,
        expert_gate[0].T, expert_up[0].T, expert_down[0],
    )
    gpg, upg, dwg, gg, ug, dg, mig = place(outs)
    return gpg.T, upg.T, dwg, gg.T[None], ug.T[None], dg[None], mig.T


def solution(mesh):
    in_specs = (
        P("row", "col"),
        P("row", "col"),
        P("row", "col"),
        P("row", "col"),
        P("col", "row"),
        P("row", None),
        P("row", None),
        P("row", None, "col"),
        P("row", None, "col"),
        P("row", "col", None),
    )
    out_specs = (
        P("row", "col"),
        P("row", "col"),
        P("col", "row"),
        P("row", None, "col"),
        P("row", None, "col"),
        P("row", "col", None),
        P("row", "col"),
    )
    return jax.shard_map(body, mesh=mesh, in_specs=in_specs, out_specs=out_specs, check_vma=False)
```

```python
import jax
import jax.numpy as jnp
from jax import lax
from jax.experimental import pallas as pl
from jax.experimental.pallas import tpu as pltpu
from jax.sharding import PartitionSpec as P

TOK = 1024
FEAT = 448
PAIR = 2 * FEAT
FFD = 304
HID = 152
ROWS = 8
CHIPS = 8
WIN = 4
CAP = 24
PAD = 32
SLOTS = ROWS * CAP
HALF = SLOTS // 2

F32 = jnp.float32
BF16 = jnp.bfloat16
MESH = pl.DeviceIdType.MESH

NN = (((1,), (0,)), ((), ()))
NT = (((1,), (1,)), ((), ()))
TN = (((0,), (0,)), ((), ()))


def dot(a, b, dims):
    return lax.dot_general(a, b, dims, preferred_element_type=F32)


def slope_of(values, sigma):
    return sigma * (1.0 + values * (1.0 - sigma))


class Channels:
    def __init__(self, send, recv):
        self.send, self.recv, self.used, self.sent = send, recv, 0, []

    def take(self, count=1):
        first = self.used
        self.used += count
        return first

    def copy(self, src, dst, device, index=None):
        index = self.take() if index is None else index
        return pltpu.make_async_remote_copy(
            src_ref=src,
            dst_ref=dst,
            send_sem=self.send.at[index],
            recv_sem=self.recv.at[index],
            device_id=device,
            device_id_type=MESH,
        )

    def go(self, src, dst, device):
        made = self.copy(src, dst, device)
        made.start()
        self.sent.append(made)
        return made


CHANNELS = 160


class RingPair:
    def __init__(self, ch, slot, cut, size, pos, side, right, left, across):
        self.ch, self.slot, self.cut, self.size = ch, slot, cut, size
        self.pos, self.side = pos, side
        self.right, self.left, self.across = right, left, across

    def at(self, delta, flip):
        return self.slot((self.pos + delta) % 4, (self.side + flip) % 2)

    def own_near(self, src):
        dst = self.at(0, 0)
        self.a = self.ch.go(src, dst, self.right)
        self.b = self.ch.go(src, dst, self.left)

    def own_across(self, src):
        self.c = self.ch.go(src, self.at(0, 0), self.across)

    def _far(self, flip):
        lo, hi = pl.ds(0, self.cut), pl.ds(self.cut, self.size - self.cut)
        from_left, from_right = self.at(3, flip), self.at(1, flip)
        return (
            self.ch.go(from_left.at[lo], from_left.at[lo], self.right),
            self.ch.go(from_right.at[hi], from_right.at[hi], self.left),
        )

    def near_done(self):
        self.a.wait_recv()
        self.b.wait_recv()

    def far(self):
        self.d = self._far(0)

    def across_done(self):
        self.c.wait_recv()

    def other(self):
        src = self.at(0, 1)
        self.e = (self.ch.go(src, src, self.right), self.ch.go(src, src, self.left))

    def far_done(self):
        for each in self.d:
            each.wait_recv()

    def other_done(self):
        for each in self.e:
            each.wait_recv()

    def other_far(self):
        self.f = self._far(1)

    def far_across(self):
        src = self.at(2, 0)
        self.f = (self.ch.go(src, src, self.across),)

    def all_done(self):
        for each in self.f:
            each.wait_recv()


def kernel(
    ids_ref, gates_ref, gp, up, og, li, dw, wg, wu, wd,
    gpg, upg, dwg, gg, ug, dg, mig,
    gp_ref, up_ref, panel, li_pair, dw_all, d_send, d_recv, y_recv, y_last, rows, w_gate, w_up, w_down,
    e_part, e_sib, e_sum, e_recv, c_send, c_recv, g_send, f_recv,
    picked, hidden, hg, mids, back, send_sems, recv_sems, local_sems,
):
    r = lax.axis_index("row")
    c = lax.axis_index("col")
    yl, z = r // 4, r % 4
    x, yh, k = c // 4, (c // 2) % 2, c % 2
    chip = c // 2

    def row_of(yl_, z_):
        return yl_ * 4 + z_

    def chip_of(x_, yh_):
        return x_ * 2 + yh_

    def col_dev(x_, yh_):
        return (r, chip_of(x_, yh_) * 2 + k)

    def row_dev(row_):
        return (row_, c)

    sib = (r, chip * 2 + (1 - k))

    barrier = pltpu.get_barrier_semaphore()
    greeted = 0
    for o in range(1, 8):
        pl.semaphore_signal(barrier, inc=1, device_id=row_dev((r + o) % 8), device_id_type=MESH)
        pl.semaphore_signal(
            barrier, inc=1, device_id=col_dev((x + o // 2) % 4, (yh + o % 2) % 2), device_id_type=MESH
        )
        greeted += 2
    for o in range(8):
        pl.semaphore_signal(
            barrier, inc=1, device_id=((r + o) % 8, chip * 2 + (1 - k)), device_id_type=MESH
        )
        greeted += 1
    ch = Channels(send_sems, recv_sems)
    lanes = pl.ds(pl.multiple_of(k * FEAT, FEAT), FEAT)

    def panel_slot(x_, yh_):
        return panel.at[chip_of(x_, yh_), lanes]

    def rows_slot(x_, yh_):
        return rows.at[k, chip_of(x_, yh_)]

    def dw_slot(z_, yl_):
        return dw_all.at[row_of(yl_, z_)]

    li_slot = li_pair.at[lanes]
    own_slot = panel_slot(x, yh)
    local = [
        pltpu.make_async_copy(og, own_slot, local_sems.at[0]),
        pltpu.make_async_copy(li, li_slot, local_sems.at[1]),
        pltpu.make_async_copy(dw, dw_slot(z, yl), local_sems.at[2]),
        pltpu.make_async_copy(wg, w_gate, local_sems.at[3]),
        pltpu.make_async_copy(wu, w_up, local_sems.at[4]),
        pltpu.make_async_copy(wd, w_down, local_sems.at[5]),
        pltpu.make_async_copy(gp, gp_ref, local_sems.at[10]),
        pltpu.make_async_copy(up, up_ref, local_sems.at[11]),
    ]
    for each in local:
        each.start()

    ids0, ids1 = ids_ref[0:1, :], ids_ref[1:2, :]
    expert = lax.broadcasted_iota(jnp.int32, (8, TOK), 0)
    lane = lax.broadcasted_iota(jnp.int32, (8, TOK), 1)
    first = (jnp.broadcast_to(ids0, (8, TOK)) == expert).astype(F32)
    second = (jnp.broadcast_to(ids1, (8, TOK)) == expert).astype(F32)
    hits = first + second
    ranks = hits
    step = 1
    while step < TOK:
        ranks = ranks + jnp.where(lane >= step, pltpu.roll(ranks, step, 1), 0.0)
        step *= 2
    ranks = (ranks - hits).astype(jnp.int32)
    gate_of = first * gates_ref[0:1, :] + second * gates_ref[1:2, :]
    place = lax.broadcasted_iota(jnp.int32, (PAD, TOK), 0)
    weights = []
    for e in range(WIN):
        same = jnp.broadcast_to(ranks[e : e + 1, :], (PAD, TOK)) == place
        mine = jnp.where(same & (place < CAP), jnp.broadcast_to(hits[e : e + 1, :], (PAD, TOK)), 0.0)
        picked[pl.ds(e * PAD, PAD), :] = mine.astype(BF16)
        weights.append(jnp.sum(mine * gate_of[e : e + 1, :], axis=1, keepdims=True))
    weights = jnp.concatenate(weights, axis=0)

    pl.semaphore_wait(barrier, greeted)

    x_right, x_left, y_across = col_dev((x + 1) % 4, yh), col_dev((x + 3) % 4, yh), col_dev(x, 1 - yh)
    ga = RingPair(ch, panel_slot, FEAT // 2, FEAT, x, yh, x_right, x_left, y_across)
    gc = RingPair(ch, rows_slot, HALF, SLOTS, x, yh, x_right, x_left, y_across)
    gb = RingPair(
        ch, dw_slot, 160, FFD, z, yl,
        row_dev(row_of(yl, (z + 1) % 4)), row_dev(row_of(yl, (z + 3) % 4)), row_dev(row_of(1 - yl, z)),
    )

    local[0].wait()
    local[1].wait()
    sib_og = ch.copy(own_slot, own_slot, sib)
    sib_li = ch.copy(li_slot, li_slot, sib)

    @pl.when(k == 1)
    def _():
        sib_li.start()

    sib_og.start()
    ch.sent.append(sib_og)
    ga.own_near(own_slot)
    ga.own_across(own_slot)
    sib_og.wait_recv()

    @pl.when(k == 0)
    def _():
        sib_li.wait_recv()
        chosen = dot(picked[...], li_pair[...], NT)
        c_send[...] = chosen.astype(BF16).reshape(WIN, PAD, PAIR)

    @pl.when(k == 1)
    def _():
        chosen = dot(picked[...], panel[chip], NT) * weights
        c_send[...] = chosen.astype(BF16).reshape(WIN, PAD, PAIR)

    to_experts = []
    for o in range(1, 8):
        dest = (r + o) % 8
        to_experts.append(ch.go(c_send.at[dest // 2], c_recv.at[r], row_dev(dest)))
    keep = pltpu.make_async_copy(c_send.at[r // 2], c_recv.at[r], local_sems.at[6])
    keep.start()

    local[2].wait()
    gb.own_near(dw_slot(z, yl))

    local[6].wait()
    local[7].wait()

    def hide(i, carry):
        part = pl.ds(pl.multiple_of(i * 16, 16), 16)
        v = gp_ref[part, :].astype(F32)
        hidden[part, :] = (v * jax.nn.sigmoid(v) * up_ref[part, :].astype(F32)).astype(BF16)
        return carry

    lax.fori_loop(0, FFD // 16, hide, 0)

    d_first = ch.take(16)
    d_out = ch.take(16)
    y_first = ch.take(4)
    y_out = ch.take(16)
    cuts = (pl.ds(0, 160), pl.ds(160, FFD - 160))

    def chip_at(o):
        return chip_of((x + o // 2) % 4, (yh + o % 2) % 2)

    def z_copy(j, p):
        to = (j // 4) * 4 + z
        return pltpu.make_async_remote_copy(
            src_ref=d_send.at[j, cuts[p]],
            dst_ref=d_recv.at[to, cuts[p]],
            send_sem=send_sems.at[d_out + j * 2 + p],
            recv_sem=recv_sems.at[d_first + to * 2 + p],
            device_id=row_dev(row_of(yl, j % 4)),
            device_id_type=MESH,
        )

    def z_arrival(side, source, p):
        to = side * 4 + source
        return pltpu.make_async_remote_copy(
            src_ref=d_send.at[0, cuts[p]],
            dst_ref=d_recv.at[to, cuts[p]],
            send_sem=send_sems.at[d_out + p],
            recv_sem=recv_sems.at[d_first + to * 2 + p],
            device_id=sib,
            device_id_type=MESH,
        )

    def y_copy(j, p):
        to = (j % 4) // 2
        return pltpu.make_async_remote_copy(
            src_ref=d_send.at[j, cuts[p]],
            dst_ref=y_recv.at[to, cuts[p]],
            send_sem=send_sems.at[y_out + j * 2 + p],
            recv_sem=recv_sems.at[y_first + to * 2 + p],
            device_id=row_dev(row_of(1 - yl, z)),
            device_id_type=MESH,
        )

    def down_z(o):
        j = chip_at(o)
        d_send[j] = dot(hidden[...], panel[j], NT).astype(BF16)

        @pl.when(j % 4 != z)
        def _():
            for p in range(2):
                z_copy(j, p).start()

    def down_y(o):
        j = chip_at(o)
        d_send[j] = dot(hidden[...], panel[j], NT).astype(BF16)

        @pl.when(j // 4 != yl)
        def _():
            for p in range(2):
                y_copy(j, p).start()

    def down_join(o):
        j = chip_at(o)

        @pl.when(j // 4 == yl)
        def _():
            for p in range(2):
                y_copy(j, p).wait_recv()

                def add(i, carry, p=p):
                    part = pl.ds(pl.multiple_of(p * 160 + i * 16, 16), 16)
                    total = d_send[j, part].astype(F32) + y_recv[(j % 4) // 2, part].astype(F32)
                    d_send[j, part] = total.astype(BF16)
                    return carry

                lax.fori_loop(0, 10 - p, add, 0)

                @pl.when(j % 4 != z)
                def _(p=p):
                    z_copy(j, p).start()

    def sum_z(side, part, j):
        total = d_send[j, part].astype(F32)
        for o in range(1, 4):
            total = total + d_recv[side * 4 + (z + o) % 4, part].astype(F32)
        return total

    def wait_z(side):
        for o in range(1, 4):
            for p in range(2):
                z_arrival(side, (z + o) % 4, p).wait_recv()

    across_row = row_of(1 - yl, z)
    z_mode = (z % 2 == yh) | (z // 2 == x % 2)
    y_final = ch.copy(d_send.at[across_row], y_last, row_dev(across_row))

    def down_cross():
        @pl.when(z_mode)
        def _():
            wait_z(1 - yl)

            def add_cross(i, carry):
                part = pl.ds(pl.multiple_of(i * 16, 16), 16)
                d_send[across_row, part] = sum_z(1 - yl, part, across_row).astype(BF16)
                return carry

            lax.fori_loop(0, FFD // 16, add_cross, 0)
            y_final.start()

    for each in to_experts:
        each.wait_recv()
    keep.wait()
    packed = c_recv[...].astype(F32)[:, :CAP, :].reshape(SLOTS, PAIR).astype(BF16)
    rows[k, chip] = packed
    gc_own = gc.at(0, 0)
    c_sib = {0: ch.go(gc_own, gc_own, sib)}
    gc.own_near(gc_own)
    gc.own_across(gc_own)

    def forward(gather, kept, offsets):
        for o in offsets:
            slot = gather.at(o // 2, o % 2)
            kept[o] = ch.go(slot, slot, sib)

    def lanes_of(i):
        return pl.ds(pl.multiple_of(i * PAIR, 128), PAIR)

    def enter(o):
        i = chip_at(o)
        part = lanes_of(i)
        taken = rows[0, i]
        mids[0] += dot(taken, w_gate[:, part], NT)
        mids[1] += dot(taken, w_up[:, part], NT)
        mids[2] += dot(rows[1, i], w_down[:, part], NT)

    def hidden_block(o):
        j = chip_at(o)
        hg[...] += dot(dw_all[j], panel[j], NN)

    def near_offset(i):
        return jnp.where(i == 0, 1, jnp.where(i == 1, 2, 6))

    def over(count, what, offset):
        def step(i, carry):
            what(offset(i))
            return carry

        lax.fori_loop(0, count, step, 0)

    mids[...] = jnp.zeros_like(mids)
    hg[...] = jnp.zeros_like(hg)

    a_sib = {}
    down_z(0)
    for each in local[3:6]:
        each.wait()
    c_sib[0].wait_recv()
    enter(0)
    ga.near_done()
    ga.far()
    forward(ga, a_sib, (2, 6))
    ga.across_done()
    ga.other()
    forward(ga, a_sib, (1,))
    gb.own_across(dw_slot(z, yl))
    gb.near_done()
    gb.far()
    gc.near_done()
    forward(gc, c_sib, (2, 6))
    gc.across_done()
    forward(gc, c_sib, (1,))
    for o in (2, 6):
        a_sib[o].wait_recv()
    over(2, down_z, lambda i: 2 + 4 * i)
    a_sib[1].wait_recv()
    down_z(1)
    for o in (1, 2, 6):
        c_sib[o].wait_recv()
    over(3, enter, near_offset)

    ga.far_done()
    ga.far_across()
    gc.other()
    gc.far()
    forward(ga, a_sib, (4,))
    gb.across_done()
    gb.other()
    a_sib[4].wait_recv()
    down_z(4)
    gc.far_done()
    forward(gc, c_sib, (4,))
    gb.far_done()
    c_sib[4].wait_recv()
    enter(4)
    gc.other_done()
    gc.other_far()
    forward(gc, c_sib, (3, 7))
    ga.other_done()
    forward(ga, a_sib, (3, 7))
    gb.other_done()
    gb.other_far()
    for o in (3, 7):
        a_sib[o].wait_recv()
    over(2, down_y, lambda i: 3 + 4 * i)
    for o in (3, 7):
        c_sib[o].wait_recv()
    over(2, enter, lambda i: 3 + 4 * i)
    ga.all_done()
    forward(ga, a_sib, (5,))
    gc.all_done()
    forward(gc, c_sib, (5,))
    a_sib[5].wait_recv()
    down_z(5)
    c_sib[5].wait_recv()
    enter(5)

    gate_value, up_value, inner_grad = mids[0], mids[1], mids[2]
    sigma = jax.nn.sigmoid(gate_value)
    active = gate_value * sigma
    inner = (active * up_value).astype(BF16)
    up_local = (inner_grad * active).astype(BF16)
    gate_local = (inner_grad * up_value * slope_of(gate_value, sigma)).astype(BF16)

    mine = pl.ds(pl.multiple_of(k * HALF, HALF), HALF)
    theirs = pl.ds(pl.multiple_of((1 - k) * HALF, HALF), HALF)
    between = ch.take(8)
    outward = ch.take(8)

    def to_sib(o):
        return ch.copy(e_part.at[chip_at(o), theirs], e_sib.at[o], sib, between + o)

    def to_chip(o):
        x_, yh_ = (x + o // 2) % 4, (yh + o % 2) % 2
        return ch.copy(e_sum.at[o], e_recv.at[o], col_dev(x_, yh_), outward + o)

    def leave(o):
        i = chip_at(o)
        part = lanes_of(i)
        total = dot(gate_local, w_gate[:, part], NN) + dot(up_local, w_up[:, part], NN)
        e_part[i] = total.astype(BF16)
        to_sib(o).start()

    def join(o):
        to_sib(o).wait_recv()
        e_sum[o] = (e_part[chip_at(o), mine].astype(F32) + e_sib[o].astype(F32)).astype(BF16)

    def part_out(i, carry):
        leave(6 - i)
        join(7 - i)
        to_chip(7 - i).start()
        return carry

    leave(7)
    lax.fori_loop(0, 7, part_out, 0)
    join(0)

    over(2, down_join, lambda i: 3 + 4 * i)

    gb.all_done()
    over(4, hidden_block, lambda i: i)
    down_cross()

    for o in range(1, 8):
        to_chip(o).wait_recv()
    returned = e_sum[0].astype(F32)
    for o in range(1, 8):
        returned = returned + e_recv[o].astype(F32)
    returned = returned.reshape(ROWS // 2, CAP, PAIR)
    filled = jnp.concatenate([returned, jnp.zeros((ROWS // 2, PAD - CAP, PAIR), F32)], axis=1)
    g_send[...] = filled.astype(BF16)

    home_first = ch.take(8)
    home_send = ch.take(8)

    def home_copy(i, core):
        dest = (k * 4 + i, chip * 2 + core)
        return pltpu.make_async_remote_copy(
            src_ref=g_send.at[i],
            dst_ref=f_recv.at[r],
            send_sem=send_sems.at[home_send + i * 2 + core],
            recv_sem=recv_sems.at[home_first + r],
            device_id=dest,
            device_id_type=MESH,
        )

    def home_self(i, core):
        return (k * 4 + i == r) & (core == k)

    for i in range(4):
        for core in range(2):
            @pl.when(jnp.logical_not(home_self(i, core)))
            def _(i=i, core=core):
                home_copy(i, core).start()

    @pl.when(r // 4 == k)
    def _():
        f_recv[r] = g_send[r % 4]

    def grads(i, carry):
        part = lanes_of(i)
        taken = rows[0, i]
        w_gate[:, part] = dot(gate_local, taken, TN).astype(BF16)
        w_up[:, part] = dot(up_local, taken, TN).astype(BF16)
        w_down[:, part] = dot(inner, rows[1, i], TN).astype(BF16)
        return carry

    lax.fori_loop(0, CHIPS, grads, 0)
    stores = [
        pltpu.make_async_copy(w_gate, gg, local_sems.at[7]),
        pltpu.make_async_copy(w_up, ug, local_sems.at[8]),
        pltpu.make_async_copy(w_down, dg, local_sems.at[9]),
    ]
    for each in stores:
        each.start()
    over(4, hidden_block, lambda i: 4 + i)

    def finish(i, carry):
        part = pl.ds(pl.multiple_of(i * 16, 16), 16)
        v = gp_ref[part, :].astype(F32)
        sigma = jax.nn.sigmoid(v)
        grad = hg[part, :]
        gp_ref[part, :] = (grad * up_ref[part, :].astype(F32) * slope_of(v, sigma)).astype(BF16)
        up_ref[part, :] = (grad * (v * sigma)).astype(BF16)
        return carry

    lax.fori_loop(0, FFD // 16, finish, 0)
    stores += [
        pltpu.make_async_copy(gp_ref, gpg, local_sems.at[12]),
        pltpu.make_async_copy(up_ref, upg, local_sems.at[13]),
    ]
    stores[3].start()
    stores[4].start()

    def home_arrival(source):
        return pltpu.make_async_remote_copy(
            src_ref=g_send.at[0],
            dst_ref=f_recv.at[source],
            send_sem=send_sems.at[home_send],
            recv_sem=recv_sems.at[home_first + source],
            device_id=sib,
            device_id_type=MESH,
        )

    for o in range(1, 8):
        home_arrival((r + o) % 8).wait_recv()

    @pl.when(r // 4 != k)
    def _():
        home_arrival(r).wait_recv()

    halves = f_recv[...].astype(F32).reshape(WIN, 2, PAD, PAIR)
    combined = (halves[:, 0] + halves[:, 1]).reshape(WIN * PAD, PAIR)
    back[...] = jnp.transpose(combined).astype(BF16)
    result = li_pair.at[pl.ds(0, FEAT)]
    result[...] = dot(back[lanes, :], picked[...], NN).astype(BF16)
    stores.append(pltpu.make_async_copy(result, mig, local_sems.at[14]))
    stores[5].start()

    wait_z(yl)

    @pl.when(z_mode)
    def _():
        y_final.wait_recv()

        def add_both(i, carry):
            part = pl.ds(pl.multiple_of(i * 16, 16), 16)
            d_send[r, part] = (sum_z(yl, part, r) + y_last[part, :].astype(F32)).astype(BF16)
            return carry

        lax.fori_loop(0, FFD // 16, add_both, 0)

    @pl.when(jnp.logical_not(z_mode))
    def _():
        def add_z(i, carry):
            part = pl.ds(pl.multiple_of(i * 16, 16), 16)
            d_send[r, part] = sum_z(yl, part, r).astype(BF16)
            return carry

        lax.fori_loop(0, FFD // 16, add_z, 0)

    stores.append(pltpu.make_async_copy(d_send.at[r], dwg, local_sems.at[15]))
    stores[6].start()

    for each in stores:
        each.wait()
    for each in ch.sent:
        each.wait_send()
    for o in range(8):
        to_sib(o).wait_send()
        if o:
            to_chip(o).wait_send()
    @pl.when(k == 1)
    def _():
        sib_li.wait_send()

    for j in range(8):
        in_plane = (j % 2 == yh) | ((j // 2 - x) % 2 == 0)
        to_z = (j % 4 != z) & (in_plane | (j // 4 == yl))
        to_y = jnp.logical_not(in_plane) & (j // 4 != yl)

        @pl.when(to_z)
        def _(j=j):
            for p in range(2):
                z_copy(j, p).wait_send()

        @pl.when(to_y)
        def _(j=j):
            for p in range(2):
                y_copy(j, p).wait_send()

    @pl.when(z_mode)
    def _():
        y_final.wait_send()

    for i in range(4):
        for core in range(2):
            @pl.when(jnp.logical_not(home_self(i, core)))
            def _(i=i, core=core):
                home_copy(i, core).wait_send()


def pieces(shape):
    width = shape[1] // 2 if shape[1] > 2 * TOK else shape[1]
    return [pl.ds(at, width) for at in range(0, shape[1], width)]


def place_kernel(*refs):
    count = (len(refs) - 2) // 3
    read_sems, write_sems = refs[-2:]
    pairs = []
    for src, dst, held in zip(refs[:count], refs[count : 2 * count], refs[2 * count : 3 * count]):
        for part in pieces(src.shape):
            n = len(pairs)
            pairs.append((
                pltpu.make_async_copy(src.at[:, part], held.at[:, part], read_sems.at[n]),
                pltpu.make_async_copy(held.at[:, part], dst.at[:, part], write_sems.at[n]),
            ))
    for read, _ in pairs:
        read.start()
    for read, write in pairs:
        read.wait()
        write.start()
    for _, write in pairs:
        write.wait()


def place(arrays):
    hbm = pl.BlockSpec(memory_space=pl.ANY)
    count = len(arrays)
    total = sum(len(pieces(a.shape)) for a in arrays)
    return pl.pallas_call(
        place_kernel,
        out_shape=tuple(jax.ShapeDtypeStruct(a.shape, a.dtype) for a in arrays),
        in_specs=[hbm] * count,
        out_specs=(hbm,) * count,
        scratch_shapes=[pltpu.VMEM(a.shape, a.dtype) for a in arrays]
        + [pltpu.SemaphoreType.DMA((total,)), pltpu.SemaphoreType.DMA((total,))],
        compiler_params=pltpu.CompilerParams(vmem_limit_bytes=63 * 1024 * 1024),
        name="place_results",
    )(*arrays)


def body(
    layer_input, output_grad, gate_pre, up_pre, down_weight,
    route_ids, route_gates, expert_gate, expert_up, expert_down,
):
    vmem = pl.BlockSpec(memory_space=pltpu.VMEM)
    hbm = pl.BlockSpec(memory_space=pl.ANY)

    def shape(*dims, dtype=BF16):
        return jax.ShapeDtypeStruct(dims, dtype)

    def scratch(*dims, dtype=BF16):
        return pltpu.VMEM(dims, dtype)

    outs = pl.pallas_call(
        kernel,
        out_shape=(
            shape(FFD, TOK), shape(FFD, TOK), shape(FFD, PAIR),
            shape(HID, CHIPS * PAIR), shape(HID, CHIPS * PAIR), shape(HID, CHIPS * PAIR),
            shape(FEAT, TOK),
        ),
        in_specs=[vmem] * 2 + [hbm] * 8,
        out_specs=(hbm,) * 7,
        scratch_shapes=[
            scratch(FFD, TOK),
            scratch(FFD, TOK),
            scratch(CHIPS, PAIR, TOK),
            scratch(PAIR, TOK),
            scratch(ROWS, FFD, PAIR),
            scratch(ROWS, FFD, PAIR),
            scratch(ROWS, FFD, PAIR),
            scratch(2, FFD, PAIR),
            scratch(FFD, PAIR),
            scratch(2, CHIPS, SLOTS, PAIR),
            scratch(HID, CHIPS * PAIR),
            scratch(HID, CHIPS * PAIR),
            scratch(HID, CHIPS * PAIR),
            scratch(CHIPS, SLOTS, PAIR),
            scratch(CHIPS, HALF, PAIR),
            scratch(CHIPS, HALF, PAIR),
            scratch(CHIPS, HALF, PAIR),
            scratch(WIN, PAD, PAIR),
            scratch(ROWS, PAD, PAIR),
            scratch(ROWS // 2, PAD, PAIR),
            scratch(ROWS, PAD, PAIR),
            scratch(WIN * PAD, TOK),
            scratch(FFD, TOK),
            scratch(FFD, TOK, dtype=F32),
            scratch(3, SLOTS, HID, dtype=F32),
            scratch(PAIR, WIN * PAD),
            pltpu.SemaphoreType.DMA((CHANNELS,)),
            pltpu.SemaphoreType.DMA((CHANNELS,)),
            pltpu.SemaphoreType.DMA((16,)),
        ],
        compiler_params=pltpu.CompilerParams(
            collective_id=0, has_side_effects=True, vmem_limit_bytes=63 * 1024 * 1024
        ),
        name="layer_backward",
    )(
        route_ids.T, route_gates.T, gate_pre.T, up_pre.T, output_grad.T, layer_input.T, down_weight,
        expert_gate[0].T, expert_up[0].T, expert_down[0],
    )
    gpg, upg, dwg, gg, ug, dg, mig = place(outs)
    return gpg.T, upg.T, dwg, gg.T[None], ug.T[None], dg[None], mig.T


def solution(mesh):
    in_specs = (
        P("row", "col"),
        P("row", "col"),
        P("row", "col"),
        P("row", "col"),
        P("col", "row"),
        P("row", None),
        P("row", None),
        P("row", None, "col"),
        P("row", None, "col"),
        P("row", "col", None),
    )
    out_specs = (
        P("row", "col"),
        P("row", "col"),
        P("col", "row"),
        P("row", None, "col"),
        P("row", None, "col"),
        P("row", "col", None),
        P("row", "col"),
    )
    return jax.shard_map(body, mesh=mesh, in_specs=in_specs, out_specs=out_specs, check_vma=False)
```

```python
import jax
import jax.numpy as jnp
from jax import lax
from jax.experimental import pallas as pl
from jax.experimental.pallas import tpu as pltpu
from jax.sharding import PartitionSpec as P

TOK = 1024
FEAT = 448
PAIR = 2 * FEAT
FFD = 304
HID = 152
ROWS = 8
CHIPS = 8
WIN = 4
CAP = 24
PAD = 32
SLOTS = ROWS * CAP
HALF = SLOTS // 2

F32 = jnp.float32
BF16 = jnp.bfloat16
MESH = pl.DeviceIdType.MESH

NN = (((1,), (0,)), ((), ()))
NT = (((1,), (1,)), ((), ()))
TN = (((0,), (0,)), ((), ()))


def dot(a, b, dims):
    return lax.dot_general(a, b, dims, preferred_element_type=F32)


def slope_of(values, sigma):
    return sigma * (1.0 + values * (1.0 - sigma))


class Channels:
    def __init__(self, send, recv):
        self.send, self.recv, self.used, self.sent = send, recv, 0, []

    def take(self, count=1):
        first = self.used
        self.used += count
        return first

    def copy(self, src, dst, device, index=None):
        index = self.take() if index is None else index
        return pltpu.make_async_remote_copy(
            src_ref=src,
            dst_ref=dst,
            send_sem=self.send.at[index],
            recv_sem=self.recv.at[index],
            device_id=device,
            device_id_type=MESH,
        )

    def go(self, src, dst, device):
        made = self.copy(src, dst, device)
        made.start()
        self.sent.append(made)
        return made


CHANNELS = 160


class RingPair:
    def __init__(self, ch, slot, cut, size, pos, side, right, left, across):
        self.ch, self.slot, self.cut, self.size = ch, slot, cut, size
        self.pos, self.side = pos, side
        self.right, self.left, self.across = right, left, across

    def at(self, delta, flip):
        return self.slot((self.pos + delta) % 4, (self.side + flip) % 2)

    def own_near(self, src):
        dst = self.at(0, 0)
        self.a = self.ch.go(src, dst, self.right)
        self.b = self.ch.go(src, dst, self.left)

    def own_across(self, src):
        self.c = self.ch.go(src, self.at(0, 0), self.across)

    def _far(self, flip):
        lo, hi = pl.ds(0, self.cut), pl.ds(self.cut, self.size - self.cut)
        from_left, from_right = self.at(3, flip), self.at(1, flip)
        return (
            self.ch.go(from_left.at[lo], from_left.at[lo], self.right),
            self.ch.go(from_right.at[hi], from_right.at[hi], self.left),
        )

    def near_done(self):
        self.a.wait_recv()
        self.b.wait_recv()

    def far(self):
        self.d = self._far(0)

    def across_done(self):
        self.c.wait_recv()

    def other(self):
        src = self.at(0, 1)
        self.e = (self.ch.go(src, src, self.right), self.ch.go(src, src, self.left))

    def far_done(self):
        for each in self.d:
            each.wait_recv()

    def other_done(self):
        for each in self.e:
            each.wait_recv()

    def other_far(self):
        self.f = self._far(1)

    def far_across(self):
        src = self.at(2, 0)
        self.f = (self.ch.go(src, src, self.across),)

    def all_done(self):
        for each in self.f:
            each.wait_recv()


def kernel(
    ids_ref, gates_ref, gp, up, og, li, dw, wg, wu, wd,
    gpg, upg, dwg, gg, ug, dg, mig,
    gp_ref, up_ref, panel, li_pair, dw_all, d_send, d_recv, y_recv, y_last, rows, w_gate, w_up, w_down,
    e_part, e_sib, e_sum, e_recv, c_send, c_recv, g_send, f_recv,
    picked, hidden, hg, mids, back, send_sems, recv_sems, local_sems,
):
    r = lax.axis_index("row")
    c = lax.axis_index("col")
    yl, z = r // 4, r % 4
    x, yh, k = c // 4, (c // 2) % 2, c % 2
    chip = c // 2

    def row_of(yl_, z_):
        return yl_ * 4 + z_

    def chip_of(x_, yh_):
        return x_ * 2 + yh_

    def col_dev(x_, yh_):
        return (r, chip_of(x_, yh_) * 2 + k)

    def row_dev(row_):
        return (row_, c)

    sib = (r, chip * 2 + (1 - k))

    barrier = pltpu.get_barrier_semaphore()
    greeted = 0
    for o in range(1, 8):
        pl.semaphore_signal(barrier, inc=1, device_id=row_dev((r + o) % 8), device_id_type=MESH)
        pl.semaphore_signal(
            barrier, inc=1, device_id=col_dev((x + o // 2) % 4, (yh + o % 2) % 2), device_id_type=MESH
        )
        greeted += 2
    for o in range(8):
        pl.semaphore_signal(
            barrier, inc=1, device_id=((r + o) % 8, chip * 2 + (1 - k)), device_id_type=MESH
        )
        greeted += 1
    ch = Channels(send_sems, recv_sems)
    lanes = pl.ds(pl.multiple_of(k * FEAT, FEAT), FEAT)

    def panel_slot(x_, yh_):
        return panel.at[chip_of(x_, yh_), lanes]

    def rows_slot(x_, yh_):
        return rows.at[k, chip_of(x_, yh_)]

    def dw_slot(z_, yl_):
        return dw_all.at[row_of(yl_, z_)]

    li_slot = li_pair.at[lanes]
    own_slot = panel_slot(x, yh)
    local = [
        pltpu.make_async_copy(og, own_slot, local_sems.at[0]),
        pltpu.make_async_copy(li, li_slot, local_sems.at[1]),
        pltpu.make_async_copy(dw, dw_slot(z, yl), local_sems.at[2]),
        pltpu.make_async_copy(wg, w_gate, local_sems.at[3]),
        pltpu.make_async_copy(wu, w_up, local_sems.at[4]),
        pltpu.make_async_copy(wd, w_down, local_sems.at[5]),
        pltpu.make_async_copy(gp, gp_ref, local_sems.at[10]),
        pltpu.make_async_copy(up, up_ref, local_sems.at[11]),
    ]
    for each in local:
        each.start()

    ids0, ids1 = ids_ref[0:1, :], ids_ref[1:2, :]
    expert = lax.broadcasted_iota(jnp.int32, (8, TOK), 0)
    lane = lax.broadcasted_iota(jnp.int32, (8, TOK), 1)
    first = (jnp.broadcast_to(ids0, (8, TOK)) == expert).astype(F32)
    second = (jnp.broadcast_to(ids1, (8, TOK)) == expert).astype(F32)
    hits = first + second
    ranks = hits
    step = 1
    while step < TOK:
        ranks = ranks + jnp.where(lane >= step, pltpu.roll(ranks, step, 1), 0.0)
        step *= 2
    ranks = (ranks - hits).astype(jnp.int32)
    gate_of = first * gates_ref[0:1, :] + second * gates_ref[1:2, :]
    place = lax.broadcasted_iota(jnp.int32, (PAD, TOK), 0)
    weights = []
    for e in range(WIN):
        same = jnp.broadcast_to(ranks[e : e + 1, :], (PAD, TOK)) == place
        mine = jnp.where(same & (place < CAP), jnp.broadcast_to(hits[e : e + 1, :], (PAD, TOK)), 0.0)
        picked[pl.ds(e * PAD, PAD), :] = mine.astype(BF16)
        weights.append(jnp.sum(mine * gate_of[e : e + 1, :], axis=1, keepdims=True))
    weights = jnp.concatenate(weights, axis=0)

    pl.semaphore_wait(barrier, greeted)

    x_right, x_left, y_across = col_dev((x + 1) % 4, yh), col_dev((x + 3) % 4, yh), col_dev(x, 1 - yh)
    ga = RingPair(ch, panel_slot, FEAT // 2, FEAT, x, yh, x_right, x_left, y_across)
    gc = RingPair(ch, rows_slot, HALF, SLOTS, x, yh, x_right, x_left, y_across)
    gb = RingPair(
        ch, dw_slot, 160, FFD, z, yl,
        row_dev(row_of(yl, (z + 1) % 4)), row_dev(row_of(yl, (z + 3) % 4)), row_dev(row_of(1 - yl, z)),
    )

    local[0].wait()
    local[1].wait()
    sib_og = ch.copy(own_slot, own_slot, sib)
    sib_li = ch.copy(li_slot, li_slot, sib)

    @pl.when(k == 1)
    def _():
        sib_li.start()

    sib_og.start()
    ch.sent.append(sib_og)
    ga.own_near(own_slot)
    ga.own_across(own_slot)
    sib_og.wait_recv()

    @pl.when(k == 0)
    def _():
        sib_li.wait_recv()
        chosen = dot(picked[...], li_pair[...], NT)
        c_send[...] = chosen.astype(BF16).reshape(WIN, PAD, PAIR)

    @pl.when(k == 1)
    def _():
        chosen = dot(picked[...], panel[chip], NT) * weights
        c_send[...] = chosen.astype(BF16).reshape(WIN, PAD, PAIR)

    to_experts = []
    for o in range(1, 8):
        dest = (r + o) % 8
        to_experts.append(ch.go(c_send.at[dest // 2], c_recv.at[r], row_dev(dest)))
    keep = pltpu.make_async_copy(c_send.at[r // 2], c_recv.at[r], local_sems.at[6])
    keep.start()

    local[2].wait()
    gb.own_near(dw_slot(z, yl))

    local[6].wait()
    local[7].wait()

    def hide(i, carry):
        part = pl.ds(pl.multiple_of(i * 16, 16), 16)
        v = gp_ref[part, :].astype(F32)
        hidden[part, :] = (v * jax.nn.sigmoid(v) * up_ref[part, :].astype(F32)).astype(BF16)
        return carry

    lax.fori_loop(0, FFD // 16, hide, 0)

    d_first = ch.take(16)
    d_out = ch.take(16)
    y_first = ch.take(4)
    y_out = ch.take(16)
    cuts = (pl.ds(0, 160), pl.ds(160, FFD - 160))

    def chip_at(o):
        return chip_of((x + o // 2) % 4, (yh + o % 2) % 2)

    def z_copy(j, p):
        to = (j // 4) * 4 + z
        return pltpu.make_async_remote_copy(
            src_ref=d_send.at[j, cuts[p]],
            dst_ref=d_recv.at[to, cuts[p]],
            send_sem=send_sems.at[d_out + j * 2 + p],
            recv_sem=recv_sems.at[d_first + to * 2 + p],
            device_id=row_dev(row_of(yl, j % 4)),
            device_id_type=MESH,
        )

    def z_arrival(side, source, p):
        to = side * 4 + source
        return pltpu.make_async_remote_copy(
            src_ref=d_send.at[0, cuts[p]],
            dst_ref=d_recv.at[to, cuts[p]],
            send_sem=send_sems.at[d_out + p],
            recv_sem=recv_sems.at[d_first + to * 2 + p],
            device_id=sib,
            device_id_type=MESH,
        )

    def y_copy(j, p):
        to = (j % 4) // 2
        return pltpu.make_async_remote_copy(
            src_ref=d_send.at[j, cuts[p]],
            dst_ref=y_recv.at[to, cuts[p]],
            send_sem=send_sems.at[y_out + j * 2 + p],
            recv_sem=recv_sems.at[y_first + to * 2 + p],
            device_id=row_dev(row_of(1 - yl, z)),
            device_id_type=MESH,
        )

    def down_z(o):
        j = chip_at(o)
        d_send[j] = dot(hidden[...], panel[j], NT).astype(BF16)

        @pl.when(j % 4 != z)
        def _():
            for p in range(2):
                z_copy(j, p).start()

    def down_y(o):
        j = chip_at(o)
        d_send[j] = dot(hidden[...], panel[j], NT).astype(BF16)

        @pl.when(j // 4 != yl)
        def _():
            for p in range(2):
                y_copy(j, p).start()

    def down_join(o):
        j = chip_at(o)

        @pl.when(j // 4 == yl)
        def _():
            for p in range(2):
                y_copy(j, p).wait_recv()

                def add(i, carry, p=p):
                    part = pl.ds(pl.multiple_of(p * 160 + i * 16, 16), 16)
                    total = d_send[j, part].astype(F32) + y_recv[(j % 4) // 2, part].astype(F32)
                    d_send[j, part] = total.astype(BF16)
                    return carry

                lax.fori_loop(0, 10 - p, add, 0)

                @pl.when(j % 4 != z)
                def _(p=p):
                    z_copy(j, p).start()

    def sum_z(side, part, j):
        total = d_send[j, part].astype(F32)
        for o in range(1, 4):
            total = total + d_recv[side * 4 + (z + o) % 4, part].astype(F32)
        return total

    def wait_z(side):
        for o in range(1, 4):
            for p in range(2):
                z_arrival(side, (z + o) % 4, p).wait_recv()

    across_row = row_of(1 - yl, z)
    z_mode = (z % 2 == yh) | (z // 2 == x % 2)
    y_final = [
        ch.copy(d_send.at[across_row, cut], y_last.at[cut], row_dev(across_row)) for cut in cuts
    ]

    def down_cross():
        @pl.when(z_mode)
        def _():
            for p in range(2):
                for o in range(1, 4):
                    z_arrival(1 - yl, (z + o) % 4, p).wait_recv()

                def add_cross(i, carry, p=p):
                    part = pl.ds(pl.multiple_of(p * 160 + i * 16, 16), 16)
                    d_send[across_row, part] = sum_z(1 - yl, part, across_row).astype(BF16)
                    return carry

                lax.fori_loop(0, 10 - p, add_cross, 0)
                y_final[p].start()

    for each in to_experts:
        each.wait_recv()
    keep.wait()
    packed = c_recv[...].astype(F32)[:, :CAP, :].reshape(SLOTS, PAIR).astype(BF16)
    rows[k, chip] = packed
    gc_own = gc.at(0, 0)
    c_sib = {0: ch.go(gc_own, gc_own, sib)}
    gc.own_near(gc_own)
    gc.own_across(gc_own)

    def forward(gather, kept, offsets):
        for o in offsets:
            slot = gather.at(o // 2, o % 2)
            kept[o] = ch.go(slot, slot, sib)

    def lanes_of(i):
        return pl.ds(pl.multiple_of(i * PAIR, 128), PAIR)

    def enter(o):
        i = chip_at(o)
        part = lanes_of(i)
        taken = rows[0, i]
        mids[0] += dot(taken, w_gate[:, part], NT)
        mids[1] += dot(taken, w_up[:, part], NT)
        mids[2] += dot(rows[1, i], w_down[:, part], NT)

    def hidden_block(o):
        j = chip_at(o)
        hg[...] += dot(dw_all[j], panel[j], NN)

    def near_offset(i):
        return jnp.where(i == 0, 1, jnp.where(i == 1, 2, 6))

    def over(count, what, offset):
        def step(i, carry):
            what(offset(i))
            return carry

        lax.fori_loop(0, count, step, 0)

    mids[...] = jnp.zeros_like(mids)
    hg[...] = jnp.zeros_like(hg)

    a_sib = {}
    down_z(0)
    for each in local[3:6]:
        each.wait()
    c_sib[0].wait_recv()
    enter(0)
    ga.near_done()
    ga.far()
    forward(ga, a_sib, (2, 6))
    ga.across_done()
    ga.other()
    forward(ga, a_sib, (1,))
    gb.own_across(dw_slot(z, yl))
    gb.near_done()
    gb.far()
    gc.near_done()
    forward(gc, c_sib, (2, 6))
    gc.across_done()
    forward(gc, c_sib, (1,))
    for o in (2, 6):
        a_sib[o].wait_recv()
    over(2, down_z, lambda i: 2 + 4 * i)
    a_sib[1].wait_recv()
    down_z(1)
    for o in (1, 2, 6):
        c_sib[o].wait_recv()
    over(3, enter, near_offset)

    ga.far_done()
    ga.far_across()
    gc.other()
    gc.far()
    forward(ga, a_sib, (4,))
    gb.across_done()
    gb.other()
    a_sib[4].wait_recv()
    down_z(4)
    gc.far_done()
    forward(gc, c_sib, (4,))
    gb.far_done()
    c_sib[4].wait_recv()
    enter(4)
    gc.other_done()
    gc.other_far()
    forward(gc, c_sib, (3, 7))
    ga.other_done()
    forward(ga, a_sib, (3, 7))
    gb.other_done()
    gb.other_far()
    for o in (3, 7):
        a_sib[o].wait_recv()
    over(2, down_y, lambda i: 3 + 4 * i)
    for o in (3, 7):
        c_sib[o].wait_recv()
    over(2, enter, lambda i: 3 + 4 * i)
    ga.all_done()
    forward(ga, a_sib, (5,))
    gc.all_done()
    forward(gc, c_sib, (5,))
    a_sib[5].wait_recv()
    down_z(5)
    c_sib[5].wait_recv()
    enter(5)

    gate_value, up_value, inner_grad = mids[0], mids[1], mids[2]
    sigma = jax.nn.sigmoid(gate_value)
    active = gate_value * sigma
    inner = (active * up_value).astype(BF16)
    up_local = (inner_grad * active).astype(BF16)
    gate_local = (inner_grad * up_value * slope_of(gate_value, sigma)).astype(BF16)

    mine = pl.ds(pl.multiple_of(k * HALF, HALF), HALF)
    theirs = pl.ds(pl.multiple_of((1 - k) * HALF, HALF), HALF)
    between = ch.take(8)
    outward = ch.take(8)

    def to_sib(o):
        return ch.copy(e_part.at[chip_at(o), theirs], e_sib.at[o], sib, between + o)

    def to_chip(o):
        x_, yh_ = (x + o // 2) % 4, (yh + o % 2) % 2
        return ch.copy(e_sum.at[o], e_recv.at[o], col_dev(x_, yh_), outward + o)

    def leave(o):
        i = chip_at(o)
        part = lanes_of(i)
        total = dot(gate_local, w_gate[:, part], NN) + dot(up_local, w_up[:, part], NN)
        e_part[i] = total.astype(BF16)
        to_sib(o).start()

    def join(o):
        to_sib(o).wait_recv()
        e_sum[o] = (e_part[chip_at(o), mine].astype(F32) + e_sib[o].astype(F32)).astype(BF16)

    def part_out(i, carry):
        leave(6 - i)
        join(7 - i)
        to_chip(7 - i).start()
        return carry

    leave(7)
    lax.fori_loop(0, 7, part_out, 0)
    join(0)

    over(2, down_join, lambda i: 3 + 4 * i)

    gb.all_done()
    over(4, hidden_block, lambda i: i)
    down_cross()

    for o in range(1, 8):
        to_chip(o).wait_recv()
    returned = e_sum[0].astype(F32)
    for o in range(1, 8):
        returned = returned + e_recv[o].astype(F32)
    returned = returned.reshape(ROWS // 2, CAP, PAIR)
    filled = jnp.concatenate([returned, jnp.zeros((ROWS // 2, PAD - CAP, PAIR), F32)], axis=1)
    g_send[...] = filled.astype(BF16)

    home_first = ch.take(8)
    home_send = ch.take(8)

    def home_copy(i, core):
        dest = (k * 4 + i, chip * 2 + core)
        return pltpu.make_async_remote_copy(
            src_ref=g_send.at[i],
            dst_ref=f_recv.at[r],
            send_sem=send_sems.at[home_send + i * 2 + core],
            recv_sem=recv_sems.at[home_first + r],
            device_id=dest,
            device_id_type=MESH,
        )

    def home_self(i, core):
        return (k * 4 + i == r) & (core == k)

    for i in range(4):
        for core in range(2):
            @pl.when(jnp.logical_not(home_self(i, core)))
            def _(i=i, core=core):
                home_copy(i, core).start()

    @pl.when(r // 4 == k)
    def _():
        f_recv[r] = g_send[r % 4]

    def grads(i, carry):
        part = lanes_of(i)
        taken = rows[0, i]
        w_gate[:, part] = dot(gate_local, taken, TN).astype(BF16)
        w_up[:, part] = dot(up_local, taken, TN).astype(BF16)
        w_down[:, part] = dot(inner, rows[1, i], TN).astype(BF16)
        return carry

    lax.fori_loop(0, CHIPS, grads, 0)
    stores = [
        pltpu.make_async_copy(w_gate, gg, local_sems.at[7]),
        pltpu.make_async_copy(w_up, ug, local_sems.at[8]),
        pltpu.make_async_copy(w_down, dg, local_sems.at[9]),
    ]
    for each in stores:
        each.start()
    over(4, hidden_block, lambda i: 4 + i)

    def finish(i, carry):
        part = pl.ds(pl.multiple_of(i * 16, 16), 16)
        v = gp_ref[part, :].astype(F32)
        sigma = jax.nn.sigmoid(v)
        grad = hg[part, :]
        gp_ref[part, :] = (grad * up_ref[part, :].astype(F32) * slope_of(v, sigma)).astype(BF16)
        up_ref[part, :] = (grad * (v * sigma)).astype(BF16)
        return carry

    lax.fori_loop(0, FFD // 16, finish, 0)
    stores += [
        pltpu.make_async_copy(gp_ref, gpg, local_sems.at[12]),
        pltpu.make_async_copy(up_ref, upg, local_sems.at[13]),
    ]
    stores[3].start()
    stores[4].start()

    def home_arrival(source):
        return pltpu.make_async_remote_copy(
            src_ref=g_send.at[0],
            dst_ref=f_recv.at[source],
            send_sem=send_sems.at[home_send],
            recv_sem=recv_sems.at[home_first + source],
            device_id=sib,
            device_id_type=MESH,
        )

    for o in range(1, 8):
        home_arrival((r + o) % 8).wait_recv()

    @pl.when(r // 4 != k)
    def _():
        home_arrival(r).wait_recv()

    halves = f_recv[...].astype(F32).reshape(WIN, 2, PAD, PAIR)
    combined = (halves[:, 0] + halves[:, 1]).reshape(WIN * PAD, PAIR)
    back[...] = jnp.transpose(combined).astype(BF16)
    result = li_pair.at[pl.ds(0, FEAT)]
    result[...] = dot(back[lanes, :], picked[...], NN).astype(BF16)
    stores.append(pltpu.make_async_copy(result, mig, local_sems.at[14]))
    stores[5].start()

    wait_z(yl)

    @pl.when(z_mode)
    def _():
        for each in y_final:
            each.wait_recv()

        def add_both(i, carry):
            part = pl.ds(pl.multiple_of(i * 16, 16), 16)
            d_send[r, part] = (sum_z(yl, part, r) + y_last[part, :].astype(F32)).astype(BF16)
            return carry

        lax.fori_loop(0, FFD // 16, add_both, 0)

    @pl.when(jnp.logical_not(z_mode))
    def _():
        def add_z(i, carry):
            part = pl.ds(pl.multiple_of(i * 16, 16), 16)
            d_send[r, part] = sum_z(yl, part, r).astype(BF16)
            return carry

        lax.fori_loop(0, FFD // 16, add_z, 0)

    stores.append(pltpu.make_async_copy(d_send.at[r], dwg, local_sems.at[15]))
    stores[6].start()

    for each in stores:
        each.wait()
    for each in ch.sent:
        each.wait_send()
    for o in range(8):
        to_sib(o).wait_send()
        if o:
            to_chip(o).wait_send()
    @pl.when(k == 1)
    def _():
        sib_li.wait_send()

    for j in range(8):
        in_plane = (j % 2 == yh) | ((j // 2 - x) % 2 == 0)
        to_z = (j % 4 != z) & (in_plane | (j // 4 == yl))
        to_y = jnp.logical_not(in_plane) & (j // 4 != yl)

        @pl.when(to_z)
        def _(j=j):
            for p in range(2):
                z_copy(j, p).wait_send()

        @pl.when(to_y)
        def _(j=j):
            for p in range(2):
                y_copy(j, p).wait_send()

    @pl.when(z_mode)
    def _():
        for each in y_final:
            each.wait_send()

    for i in range(4):
        for core in range(2):
            @pl.when(jnp.logical_not(home_self(i, core)))
            def _(i=i, core=core):
                home_copy(i, core).wait_send()


def pieces(shape):
    width = shape[1] // 2 if shape[1] > 2 * TOK else shape[1]
    return [pl.ds(at, width) for at in range(0, shape[1], width)]


def place_kernel(*refs):
    count = (len(refs) - 2) // 3
    read_sems, write_sems = refs[-2:]
    pairs = []
    for src, dst, held in zip(refs[:count], refs[count : 2 * count], refs[2 * count : 3 * count]):
        for part in pieces(src.shape):
            n = len(pairs)
            pairs.append((
                pltpu.make_async_copy(src.at[:, part], held.at[:, part], read_sems.at[n]),
                pltpu.make_async_copy(held.at[:, part], dst.at[:, part], write_sems.at[n]),
            ))
    for read, _ in pairs:
        read.start()
    for read, write in pairs:
        read.wait()
        write.start()
    for _, write in pairs:
        write.wait()


def place(arrays):
    hbm = pl.BlockSpec(memory_space=pl.ANY)
    count = len(arrays)
    total = sum(len(pieces(a.shape)) for a in arrays)
    return pl.pallas_call(
        place_kernel,
        out_shape=tuple(jax.ShapeDtypeStruct(a.shape, a.dtype) for a in arrays),
        in_specs=[hbm] * count,
        out_specs=(hbm,) * count,
        scratch_shapes=[pltpu.VMEM(a.shape, a.dtype) for a in arrays]
        + [pltpu.SemaphoreType.DMA((total,)), pltpu.SemaphoreType.DMA((total,))],
        compiler_params=pltpu.CompilerParams(vmem_limit_bytes=63 * 1024 * 1024),
        name="place_results",
    )(*arrays)


def body(
    layer_input, output_grad, gate_pre, up_pre, down_weight,
    route_ids, route_gates, expert_gate, expert_up, expert_down,
):
    vmem = pl.BlockSpec(memory_space=pltpu.VMEM)
    hbm = pl.BlockSpec(memory_space=pl.ANY)

    def shape(*dims, dtype=BF16):
        return jax.ShapeDtypeStruct(dims, dtype)

    def scratch(*dims, dtype=BF16):
        return pltpu.VMEM(dims, dtype)

    outs = pl.pallas_call(
        kernel,
        out_shape=(
            shape(FFD, TOK), shape(FFD, TOK), shape(FFD, PAIR),
            shape(HID, CHIPS * PAIR), shape(HID, CHIPS * PAIR), shape(HID, CHIPS * PAIR),
            shape(FEAT, TOK),
        ),
        in_specs=[vmem] * 2 + [hbm] * 8,
        out_specs=(hbm,) * 7,
        scratch_shapes=[
            scratch(FFD, TOK),
            scratch(FFD, TOK),
            scratch(CHIPS, PAIR, TOK),
            scratch(PAIR, TOK),
            scratch(ROWS, FFD, PAIR),
            scratch(ROWS, FFD, PAIR),
            scratch(ROWS, FFD, PAIR),
            scratch(2, FFD, PAIR),
            scratch(FFD, PAIR),
            scratch(2, CHIPS, SLOTS, PAIR),
            scratch(HID, CHIPS * PAIR),
            scratch(HID, CHIPS * PAIR),
            scratch(HID, CHIPS * PAIR),
            scratch(CHIPS, SLOTS, PAIR),
            scratch(CHIPS, HALF, PAIR),
            scratch(CHIPS, HALF, PAIR),
            scratch(CHIPS, HALF, PAIR),
            scratch(WIN, PAD, PAIR),
            scratch(ROWS, PAD, PAIR),
            scratch(ROWS // 2, PAD, PAIR),
            scratch(ROWS, PAD, PAIR),
            scratch(WIN * PAD, TOK),
            scratch(FFD, TOK),
            scratch(FFD, TOK, dtype=F32),
            scratch(3, SLOTS, HID, dtype=F32),
            scratch(PAIR, WIN * PAD),
            pltpu.SemaphoreType.DMA((CHANNELS,)),
            pltpu.SemaphoreType.DMA((CHANNELS,)),
            pltpu.SemaphoreType.DMA((16,)),
        ],
        compiler_params=pltpu.CompilerParams(
            collective_id=0, has_side_effects=True, vmem_limit_bytes=63 * 1024 * 1024
        ),
        name="layer_backward",
    )(
        route_ids.T, route_gates.T, gate_pre.T, up_pre.T, output_grad.T, layer_input.T, down_weight,
        expert_gate[0].T, expert_up[0].T, expert_down[0],
    )
    gpg, upg, dwg, gg, ug, dg, mig = place(outs)
    return gpg.T, upg.T, dwg, gg.T[None], ug.T[None], dg[None], mig.T


def solution(mesh):
    in_specs = (
        P("row", "col"),
        P("row", "col"),
        P("row", "col"),
        P("row", "col"),
        P("col", "row"),
        P("row", None),
        P("row", None),
        P("row", None, "col"),
        P("row", None, "col"),
        P("row", "col", None),
    )
    out_specs = (
        P("row", "col"),
        P("row", "col"),
        P("col", "row"),
        P("row", None, "col"),
        P("row", None, "col"),
        P("row", "col", None),
        P("row", "col"),
    )
    return jax.shard_map(body, mesh=mesh, in_specs=in_specs, out_specs=out_specs, check_vma=False)
```
